32 devices in a mesh: req: 16 (over z, y, x), head: 2 (over core).
Axes of the slice: x: 2, y: 2, z: 4, core: 2. Of those that a mesh axis runs over, the one named last changes fastest.
Arguments:
- hidden_in: bfloat16 [1024, 2048], P('req'), may hold values from -14 to 14
- attn_gain: float32 [2048], replicated, may hold values from 0.1 to 1.9
- w_query: bfloat16 [2048, 2048], P(None, 'head'), may hold values from -0.125 to 0.125
- w_key: bfloat16 [2048, 1024], P(None, 'head'), may hold values from -0.125 to 0.125
- w_value: bfloat16 [2048, 1024], P(None, 'head'), may hold values from -0.125 to 0.125
- query_gain: float32 [128], replicated, may hold values from 0.5 to 2
- key_gain: float32 [128], replicated, may hold values from 0.5 to 2
- w_out: bfloat16 [2048, 2048], P('head'), may hold values from -0.125 to 0.125
- cache_keys: bfloat16 [16, 2048, 1024], P('req', None, 'head'), may hold values from -3.5 to 3.5
- cache_values: bfloat16 [16, 2048, 1024], P('req', None, 'head'), may hold values from -6 to 6
- cache_lengths: int32 [16], replicated, may hold values from 1 to 2048, 16384 in all
- slot_request: int32 [16], replicated, may hold values from 0 to 15, each once
- mlp_gain: float32 [2048], P('head'), may hold values from 0.1 to 1.9
- w_gate: bfloat16 [2048, 6144], P('head', 'req'), may hold values from -0.125 to 0.125
- w_up: bfloat16 [2048, 6144], P('head', 'req'), may hold values from -0.125 to 0.125
- w_down: bfloat16 [6144, 2048], P('req', 'head'), may hold values from -0.078125 to 0.078125
- final_gain: float32 [2048], replicated, may hold values from 0.1 to 1.9
- w_vocab: bfloat16 [2048, 151936], P(None, ('req', 'head')), may hold values from -8 to 8
Outputs:
- hidden_out: bfloat16 [1024, 2048], P('req', 'head')
- log_probs: float32 [16, 151936], P(None, ('req', 'head'))
The draws below stay inside these ranges and needn't reach their ends.
Inputs may be any that keep to these rules, and one draw needn't show every extreme that they name: `cache_lengths`: the largest length is exactly 2048. `slot_request`: each request appears once.
All inputs are finite; a program needn't handle non-finite values.
Results may differ from the reference program's by a relative error of at most 0.008.
Values may be sent and summed in bfloat16 or wider, within the bound.
No kernel may reach another device: no remote copies, remote signals or barrier semaphores. Data moves between devices by JAX's collectives and lax.ppermute only.
A program may use at most 128 MiB of HBM per device.

```python
import math
import jax
import jax.numpy as jnp
import numpy as np
from jax import lax

D = 2048
HEADS_Q = 16
HEADS_KV = 8
HEAD_DIM = 128
FF = 6144
VOCAB = 151936
S_NEW = 64
LMAX = 2048
REQS = 16


def draw_w_vocab(key, part):
    normal_key, scale_key = jax.random.split(key)
    entries = jax.random.truncated_normal(normal_key, -4.0, 4.0, (D, VOCAB), jnp.float32)
    spread = jax.random.uniform(scale_key, (1, VOCAB), jnp.float32, 0.0, math.log(10.0))
    return jnp.clip(entries * jnp.exp(spread) * D ** (-0.5), -8.0, 8.0).astype(jnp.bfloat16)


def draw_hidden_in(key, part):
    entry_key = jax.random.fold_in(key, 17)
    columns = jnp.arange(D, dtype=jnp.float32) / (D - 1)
    entries = jax.random.truncated_normal(entry_key, -4.0, 4.0, (REQS * S_NEW, D), jnp.float32)
    column_scale = jnp.exp(math.log(3.5) * columns)
    return jnp.clip(entries * column_scale[None, :], -14.0, 14.0).astype(jnp.bfloat16)


def shard_levels(key, dims, cuts, least, largest):
    level, own = 1.0, jax.random.fold_in(key, 6)
    for axis_at, shards_of in cuts:
        draws = jnp.exp(jax.random.uniform(jax.random.fold_in(own, axis_at), (shards_of,), jnp.float32, least / len(cuts), largest / len(cuts)))
        level = level * jnp.repeat(draws, dims[axis_at] // shards_of).reshape([-1 if axis == axis_at else 1 for axis in range(len(dims))])
    return level


def split_up(count, total, bound, slope):
    weights = [(1 << 20) // math.isqrt(grade ** slope) + 1 for grade in range(2, count + 1)]
    spare, holding = total - bound - (count - 1), [1] * (count - 1)
    while spare > 0:
        free = [i for i in range(count - 1) if holding[i] < bound]
        pool, remaining = sum([weights[i] for i in free]), spare
        for i in free:
            extra = min(bound - holding[i], max(1, remaining * weights[i] // pool), spare)
            holding[i] = holding[i] + extra
            spare = spare - extra
    return np.array([bound] + holding)


def ragged(rng, amount, total, reach, skew):
    if amount == 2:
        one = jax.random.randint(rng, (), max(1, total - reach), min(reach, total - 1) + 1)
        return jnp.stack([one, total - one])
    sizes = jnp.asarray(split_up(amount, total, reach, skew), jnp.int32)
    twos = (amount - 1) // 2
    donor, sink = sizes[1:1 + 2 * twos:2], sizes[2:2 + 2 * twos:2]
    slack = jnp.minimum(donor - 1, reach - sink)
    shifted = jax.random.randint(jax.random.fold_in(rng, 1), (twos,), 0, 1 << 20) % (slack + 1)
    sizes = sizes.at[1:1 + 2 * twos:2].set(donor - shifted).at[2:2 + 2 * twos:2].set(sink + shifted)
    return sizes[jax.random.permutation(jax.random.fold_in(rng, 2), amount)]


def noise(rng, dims, deviation, reach, cuts=(), kind=jnp.bfloat16):
    array = jax.random.normal(rng, dims, jnp.float32) * deviation
    if len(cuts) > 0:
        array = shard_levels(rng, dims, cuts, -0.22, 0.18) * array
    return jnp.clip(array, min=-reach, max=reach).astype(kind)


def setup_inputs(seed: int = 0) -> dict:
    arg_keys = jax.random.split(jax.random.key(seed), 19)
    return {
        "hidden_in": draw_hidden_in(jax.random.fold_in(arg_keys[18], 71), 0),
        "attn_gain": jnp.clip(1.0 + 0.18 * jax.random.normal(arg_keys[1], (D,), jnp.float32), 0.1, 1.9),
        "w_query": noise(arg_keys[2], (D, HEADS_Q * HEAD_DIM), D ** -0.5, 0.125, ((1, 2),)),
        "w_key": noise(arg_keys[3], (D, HEADS_KV * HEAD_DIM), D ** -0.5, 0.125, ((1, 2),)),
        "w_value": noise(arg_keys[4], (D, HEADS_KV * HEAD_DIM), D ** -0.5, 0.125, ((1, 2),)),
        "query_gain": jnp.clip(jnp.exp(jax.random.uniform(arg_keys[5], (HEAD_DIM,), jnp.float32, math.log(0.5), math.log(2.0))), 0.5, 2.0),
        "key_gain": jnp.clip(jnp.exp(jax.random.uniform(arg_keys[6], (HEAD_DIM,), jnp.float32, math.log(0.5), math.log(2.0))), 0.5, 2.0),
        "w_out": noise(arg_keys[7], (HEADS_Q * HEAD_DIM, D), (HEADS_Q * HEAD_DIM) ** -0.5, 0.125, ((0, 2),)),
        "cache_keys": noise(arg_keys[8], (REQS, LMAX, HEADS_KV * HEAD_DIM), 1.0, 3.5, ((0, 16), (2, 2))),
        "cache_values": noise(arg_keys[9], (REQS, LMAX, HEADS_KV * HEAD_DIM), 1.0, 6.0, ((0, 16), (2, 2))),
        "cache_lengths": ragged(arg_keys[10], REQS, REQS * LMAX // 2, LMAX, 2).astype(jnp.int32),
        "slot_request": jax.random.permutation(arg_keys[11], REQS).astype(jnp.int32),
        "mlp_gain": jnp.clip(1.0 + 0.18 * jax.random.normal(arg_keys[12], (D,), jnp.float32), 0.1, 1.9),
        "w_gate": noise(arg_keys[13], (D, FF), D ** -0.5, 0.125, ((0, 2), (1, 16))),
        "w_up": noise(arg_keys[14], (D, FF), D ** -0.5, 0.125, ((0, 2), (1, 16))),
        "w_down": noise(arg_keys[15], (FF, D), FF ** -0.5, 0.078125, ((0, 16), (1, 2))),
        "final_gain": jnp.clip(1.0 + 0.18 * jax.random.normal(arg_keys[16], (D,), jnp.float32), 0.1, 1.9),
        "w_vocab": draw_w_vocab(jax.random.fold_in(arg_keys[18], 71), 0),
    }


EPS = 1e-06
ROPE_BASE = 1000000.0
NEG = -1e+30

def norm_rows(field, gain_vec):
    return field * lax.rsqrt(lax.optimization_barrier(jnp.mean(field * field, axis=-1, keepdims=True)) + EPS) * gain_vec

def rotate(field, positions):
    half_dim = field.shape[-1] // 2
    frequency = ROPE_BASE ** (-2.0 * jnp.arange(half_dim, dtype=jnp.float32) / field.shape[-1])
    angles = positions[..., None, None] * frequency
    cosine = jnp.cos(angles)
    sines = jnp.sin(angles)
    lower_half = field[..., :half_dim]
    upper_half = field[..., half_dim:]
    return jnp.concatenate([lower_half * cosine - upper_half * sines, upper_half * cosine + lower_half * sines], axis=-1)

def inverse_order(slot_request):
    indices = jnp.arange(slot_request.shape[0], dtype=jnp.int32)
    return lax.optimization_barrier(jnp.sum(jnp.where(slot_request[None, :] == indices[:, None], indices[None, :], 0), axis=1)).astype(jnp.int32)

def slot_attention(inputs):
    queries, keys_new, values_new, keys_cache, values_cache, cache_len = inputs
    group_size = HEADS_Q // HEADS_KV
    grouped = queries.astype(jnp.float32).reshape(S_NEW, HEADS_KV, group_size, HEAD_DIM)
    stored_keys = keys_cache.astype(jnp.float32).reshape(LMAX, HEADS_KV, HEAD_DIM)
    stored_values = values_cache.astype(jnp.float32).reshape(LMAX, HEADS_KV, HEAD_DIM)
    score_scale = HEAD_DIM ** (-0.5)
    stored = jnp.einsum('skgd,lkd->kgsl', grouped, stored_keys) * score_scale
    stored = jnp.where(jnp.arange(LMAX, dtype=jnp.int32) < cache_len, stored, NEG)
    recent = jnp.einsum('skgd,tkd->kgst', grouped, keys_new.astype(jnp.float32)) * score_scale
    causal = jnp.arange(S_NEW)[:, None] >= jnp.arange(S_NEW)[None, :]
    recent = jnp.where(causal, recent, NEG)
    old_weights = jnp.exp(stored)
    new_weights = jnp.exp(recent)
    row_total = lax.optimization_barrier(jnp.sum(old_weights, axis=-1)) + lax.optimization_barrier(jnp.sum(new_weights, axis=-1))
    old_weights = (old_weights / row_total[..., None]).astype(jnp.bfloat16)
    new_weights = (new_weights / row_total[..., None]).astype(jnp.bfloat16)
    blended = jnp.einsum('kgsl,lkd->skgd', old_weights.astype(jnp.float32), stored_values)
    blended = blended + jnp.einsum('kgst,tkd->skgd', new_weights.astype(jnp.float32), values_new.astype(jnp.float32))
    return blended.reshape(S_NEW, HEADS_Q * HEAD_DIM).astype(jnp.bfloat16)

def reference(hidden_in, attn_gain, w_query, w_key, w_value, query_gain, key_gain, w_out, cache_keys, cache_values, cache_lengths, slot_request, mlp_gain, w_gate, w_up, w_down, final_gain, w_vocab):
    tokens = hidden_in.astype(jnp.float32)
    normed = norm_rows(tokens, attn_gain).astype(jnp.bfloat16)
    lengths = jnp.take(cache_lengths, slot_request).astype(jnp.int32)
    positions = (lengths[:, None] + jnp.arange(S_NEW, dtype=jnp.int32)[None, :]).astype(jnp.float32)
    queries = jnp.dot(normed, w_query, preferred_element_type=jnp.float32).reshape(REQS, S_NEW, HEADS_Q, HEAD_DIM)
    queries = rotate(norm_rows(queries, query_gain), positions).astype(jnp.bfloat16)
    keys_new = jnp.dot(normed, w_key, preferred_element_type=jnp.float32).reshape(REQS, S_NEW, HEADS_KV, HEAD_DIM)
    keys_new = rotate(norm_rows(keys_new, key_gain), positions).astype(jnp.bfloat16)
    values_new = jnp.dot(normed, w_value, preferred_element_type=jnp.float32).astype(jnp.bfloat16).reshape(REQS, S_NEW, HEADS_KV, HEAD_DIM)
    attended = lax.map(slot_attention, (queries, keys_new, values_new, cache_keys, cache_values, lengths))
    attended = attended.reshape(REQS * S_NEW, HEADS_Q * HEAD_DIM)
    residual = tokens + jnp.dot(attended, w_out, preferred_element_type=jnp.float32)
    mixed_rows = norm_rows(residual, mlp_gain).astype(jnp.bfloat16)
    gate_part = jnp.dot(mixed_rows, w_gate, preferred_element_type=jnp.float32)
    up_part = jnp.dot(mixed_rows, w_up, preferred_element_type=jnp.float32)
    active = (jax.nn.silu(gate_part) * up_part).astype(jnp.bfloat16)
    output = residual + jnp.dot(active, w_down, preferred_element_type=jnp.float32)
    hidden_out = output.astype(jnp.bfloat16)
    last_row = output.reshape(REQS, S_NEW, D)[:, S_NEW - 1, :]
    final_rows = norm_rows(last_row, final_gain).astype(jnp.bfloat16)
    logits = jnp.dot(final_rows, w_vocab, preferred_element_type=jnp.float32)
    row_max = lax.optimization_barrier(jnp.max(logits, axis=1, keepdims=True))
    row_total = lax.optimization_barrier(jnp.sum(jnp.exp(logits - row_max), axis=1, keepdims=True))
    log_probs = logits - row_max - jnp.log(row_total)
    log_probs = jnp.take(log_probs, inverse_order(slot_request), axis=0)
    return (hidden_out, log_probs)
```

```python
import jax
import jax.numpy as jnp
from jax import lax
from jax.sharding import PartitionSpec as P

D = 2048
HEAD_DIM = 128


EPS = 1e-06
ROPE_BASE = 1000000.0
NEG = -1e30


def norm_rows(field, gain_vec):
    return field * lax.rsqrt(jnp.mean(field * field, axis=-1, keepdims=True) + EPS) * gain_vec


def rotate(field, positions):
    half_dim = field.shape[-1] // 2
    frequency = ROPE_BASE ** (-2.0 * jnp.arange(half_dim, dtype=jnp.float32) / field.shape[-1])
    angles = positions[..., None, None] * frequency
    cosine = jnp.cos(angles)
    sines = jnp.sin(angles)
    lower_half = field[..., :half_dim]
    upper_half = field[..., half_dim:]
    return jnp.concatenate(
        [lower_half * cosine - upper_half * sines, upper_half * cosine + lower_half * sines],
        axis=-1,
    )


def inverse_order(slot_request):
    indices = jnp.arange(slot_request.shape[0], dtype=jnp.int32)
    return jnp.sum(
        jnp.where(slot_request[None, :] == indices[:, None], indices[None, :], 0), axis=1
    )


def radices(count):
    if count == 16:
        return (4, 2, 2)
    side = round(count ** (1 / 3))
    if side**3 == count:
        return (side, side, side)
    return (count, 1, 1)


def shifted(count, digit, step):
    sizes = radices(count)
    stride = 1
    for size in sizes[digit + 1 :]:
        stride *= size
    pairs = []
    for i in range(count):
        place = i // stride % sizes[digit]
        pairs.append((i, i + ((place + step) % sizes[digit] - place) * stride))
    return pairs


def send(rows, count, digit, step):
    return lax.ppermute(rows, "req", shifted(count, digit, step))


def other_core(rows):
    return lax.ppermute(rows, "head", [(0, 1), (1, 0)])


def to_all(block):
    count = lax.axis_size("req") * lax.axis_size("head")
    return lax.all_to_all(
        jnp.broadcast_to(block[None], (count,) + block.shape), ("req", "head"), 0, 0, tiled=True
    )


def attend_slot(queries, keys_new, values_new, keys_cache, values_cache, cache_len):
    row_count, value_heads, head_size = keys_new.shape
    group_size = queries.shape[1] // value_heads
    grouped = queries.reshape(row_count, value_heads, group_size, head_size)
    score_scale = head_size ** (-0.5)
    recent = (
        jnp.einsum("skgd,tkd->kgst", grouped, keys_new, preferred_element_type=jnp.float32)
        * score_scale
    )
    causal = jnp.arange(row_count)[:, None] >= jnp.arange(row_count)[None, :]
    recent = jnp.where(causal, recent, NEG)
    cache_span = keys_cache.shape[0]
    stored = (
        jnp.einsum("skgd,lkd->kgsl", grouped, keys_cache, preferred_element_type=jnp.float32)
        * score_scale
    )
    stored = jnp.where(jnp.arange(cache_span, dtype=jnp.int32) < cache_len, stored, NEG)
    old_weights = jnp.exp(stored)
    new_weights = jnp.exp(recent)
    row_total = jnp.sum(old_weights, axis=-1) + jnp.sum(new_weights, axis=-1)
    old_weights = (old_weights / row_total[..., None]).astype(jnp.bfloat16)
    new_weights = (new_weights / row_total[..., None]).astype(jnp.bfloat16)
    blended = jnp.einsum(
        "kgsl,lkd->skgd", old_weights, values_cache, preferred_element_type=jnp.float32
    )
    blended = blended + jnp.einsum(
        "kgst,tkd->skgd", new_weights, values_new, preferred_element_type=jnp.float32
    )
    return blended.reshape(row_count, value_heads * group_size * head_size).astype(jnp.bfloat16)


def feed_forward(rows, paired, w_down):
    partial_rows = jnp.dot(rows, paired, preferred_element_type=jnp.float32)
    summed = partial_rows + other_core(partial_rows.astype(jnp.bfloat16)).astype(jnp.float32)
    unit_count = w_down.shape[0]
    active = (jax.nn.silu(summed[:, :unit_count]) * summed[:, unit_count:]).astype(jnp.bfloat16)
    return jnp.dot(active, w_down, preferred_element_type=jnp.float32)


def spread_feed_forward(mixed_rows, paired, w_down):
    count = lax.axis_size("req")
    sizes = radices(count)
    row_count = mixed_rows.shape[0]
    levels = [mixed_rows] + [send(mixed_rows, count, 0, step) for step in range(1, sizes[0])]
    half = max(1, sizes[0] // 2)
    groups = [(levels[:half], 2, 1), (levels[half:], 1, 2)]
    back = []
    for blocks, first, second in groups:
        if not blocks:
            continue
        held = jnp.concatenate(blocks, axis=0)
        held = jnp.concatenate(
            [held] + [send(held, count, first, step) for step in range(1, sizes[first])], axis=0
        )
        farther = [send(held, count, second, step) for step in range(1, sizes[second])]
        near = feed_forward(held, paired, w_down)
        for step, rows in enumerate(farther, 1):
            part = feed_forward(rows, paired, w_down).astype(jnp.bfloat16)
            near = near + send(part, count, second, -step).astype(jnp.float32)
        width = len(blocks) * row_count
        total = near[:width]
        for step in range(1, sizes[first]):
            part = near[step * width : (step + 1) * width].astype(jnp.bfloat16)
            total = total + send(part, count, first, -step).astype(jnp.float32)
        back += [total[i * row_count : (i + 1) * row_count] for i in range(len(blocks))]
    result = back[0]
    for step in range(1, sizes[0]):
        result = result + send(back[step].astype(jnp.bfloat16), count, 0, -step).astype(jnp.float32)
    return result


def on_device(
    hidden_in,
    attn_gain,
    w_query,
    w_key,
    w_value,
    query_gain,
    key_gain,
    w_out,
    cache_keys,
    cache_values,
    cache_lengths,
    slot_request,
    mlp_gain,
    w_gate,
    w_up,
    w_down,
    final_gain,
    w_vocab,
):
    row_count = hidden_in.shape[0]
    half_width = mlp_gain.shape[0]
    slot_index = lax.axis_index("req")
    request_id = lax.dynamic_index_in_dim(slot_request, slot_index, 0, keepdims=False)
    cache_len = lax.dynamic_index_in_dim(cache_lengths, request_id, 0, keepdims=False)
    tokens = hidden_in.astype(jnp.float32)
    normed = norm_rows(tokens, attn_gain).astype(jnp.bfloat16)
    query_heads = w_query.shape[1] // HEAD_DIM
    value_heads = w_key.shape[1] // HEAD_DIM
    positions = (cache_len + jnp.arange(row_count, dtype=jnp.int32)).astype(jnp.float32)
    queries = jnp.dot(normed, w_query, preferred_element_type=jnp.float32).reshape(
        row_count, query_heads, HEAD_DIM
    )
    queries = rotate(norm_rows(queries, query_gain), positions).astype(jnp.bfloat16)
    keys_new = jnp.dot(normed, w_key, preferred_element_type=jnp.float32).reshape(
        row_count, value_heads, HEAD_DIM
    )
    keys_new = rotate(norm_rows(keys_new, key_gain), positions).astype(jnp.bfloat16)
    values_new = (
        jnp.dot(normed, w_value, preferred_element_type=jnp.float32)
        .astype(jnp.bfloat16)
        .reshape(row_count, value_heads, HEAD_DIM)
    )
    keys_cache = cache_keys.reshape(cache_keys.shape[1], value_heads, HEAD_DIM)
    values_cache = cache_values.reshape(cache_values.shape[1], value_heads, HEAD_DIM)
    attended = attend_slot(queries, keys_new, values_new, keys_cache, values_cache, cache_len)
    projected = jnp.dot(attended, w_out, preferred_element_type=jnp.float32)
    both = tokens + projected + other_core(projected.astype(jnp.bfloat16)).astype(jnp.float32)
    inverse = lax.rsqrt(jnp.mean(both * both, axis=1, keepdims=True) + EPS)
    head_part = lax.axis_index("head")
    residual = lax.dynamic_slice_in_dim(both, head_part * half_width, half_width, 1)
    mixed_rows = (residual * inverse * mlp_gain).astype(jnp.bfloat16)
    paired = jnp.concatenate([w_gate, w_up], axis=1)
    output = residual + spread_feed_forward(mixed_rows, paired, w_down)
    hidden_out = output.astype(jnp.bfloat16)
    last_row = output[row_count - 1 :, :].reshape(8, half_width // 8)
    collected = to_all(last_row).reshape(-1, D)
    collected = jnp.take(collected, inverse_order(slot_request), axis=0)
    final_rows = norm_rows(collected, final_gain).astype(jnp.bfloat16)
    logits = jnp.dot(final_rows, w_vocab, preferred_element_type=jnp.float32)
    own_max = jnp.max(logits, axis=1)
    own_total = jnp.sum(jnp.exp(logits - own_max[:, None]), axis=1)
    requests = own_max.shape[0]
    stats = jnp.zeros((8, 128), jnp.float32).at[0, :requests].set(own_max).at[1, :requests].set(own_total)
    everyone = to_all(stats)
    row_max = jnp.max(everyone[:, 0, :requests], axis=0)
    row_total = jnp.sum(
        everyone[:, 1, :requests] * jnp.exp(everyone[:, 0, :requests] - row_max[None, :]), axis=0
    )
    log_probs = logits - (row_max + jnp.log(row_total))[:, None]
    return (hidden_out, log_probs)


def solution(mesh):
    in_specs = (
        P("req", None),
        P(),
        P(None, "head"),
        P(None, "head"),
        P(None, "head"),
        P(),
        P(),
        P("head", None),
        P("req", None, "head"),
        P("req", None, "head"),
        P(),
        P(),
        P("head"),
        P("head", "req"),
        P("head", "req"),
        P("req", "head"),
        P(),
        P(None, ("req", "head")),
    )
    out_specs = (P("req", "head"), P(None, ("req", "head")))
    return jax.shard_map(
        on_device, mesh=mesh, in_specs=in_specs, out_specs=out_specs, check_vma=False
    )
```

```python
import jax
import jax.numpy as jnp
import numpy as np
from jax import lax
from jax.experimental import pallas as pl
from jax.experimental.pallas import tpu as pltpu
from jax.sharding import PartitionSpec as P


HEAD_DIM = 128


EPS = 1e-06
ROPE_BASE = 1000000.0
NEG = -1e30
WEIGHT = 20000000000
VMEM_SPEC = pl.BlockSpec(memory_space=pltpu.VMEM)
LOG2E = 1.4426950408889634
SHIFT = 4.0
QUERY_PARTS, CACHE_PARTS, OUT_PARTS = 4, 4, 4


def sizes_of(count):
    if count == 16:
        return (4, 2, 2)
    side = round(count ** (1 / 3))
    if side**3 == count:
        return (side, side, side)
    return (count, 1, 1)


def send(rows, count, steps):
    sizes = sizes_of(count)
    pairs = []
    for i in range(count):
        target, left = 0, i
        places = []
        for size in reversed(sizes):
            places.append(left % size)
            left //= size
        for place, size, step in zip(reversed(places), sizes, steps):
            target = target * size + (place + step) % size
        pairs.append((i, target))
    return lax.ppermute(rows, "req", pairs)


def along(count, digit):
    steps = []
    for step in range(1, sizes_of(count)[digit]):
        one = [0, 0, 0]
        one[digit] = step
        steps.append(tuple(one))
    return steps


def across(count):
    return [(0, b[1], c[2]) for b in along(count, 1) for c in along(count, 2)]


def add_steps(one, two):
    return tuple(a + b for a, b in zip(one, two))


def slot_behind(slot, count, steps):
    result, stride = 0, 1
    for size, step in zip(reversed(sizes_of(count)), reversed(steps)):
        result = result + lax.rem(lax.div(slot, stride) + size - step % size, size) * stride
        stride *= size
    return result


def back(steps):
    return tuple(-step for step in steps)


def other_core(rows):
    return lax.ppermute(rows, "head", [(0, 1), (1, 0)])


def to_all(block, names):
    count = lax.axis_size(names)
    return lax.all_to_all(jnp.broadcast_to(block[None], (count,) + block.shape), names, 0, 0, tiled=True)


def kernel_call(body, outs, flops, name, *operands, gates=()):
    def run(*refs):
        body(*refs[: len(operands)], *refs[len(operands) + len(gates) :])

    result = pl.pallas_call(
        run,
        out_shape=tuple(pltpu.VMEM(shape, dtype) for shape, dtype in outs),
        in_specs=[VMEM_SPEC] * len(operands) + [pl.BlockSpec(memory_space=pl.ANY)] * len(gates),
        out_specs=(VMEM_SPEC,) * len(outs),
        compiler_params=pltpu.CompilerParams(vmem_limit_bytes=20 * 1024 * 1024),
        cost_estimate=pl.CostEstimate(flops=flops, bytes_accessed=1000000, transcendentals=0),
        name=name,
    )(*operands, *gates)
    return result


def attention_kernel(
    lengths_any,
    requests_any,
    hidden_any,
    attn_gain_any,
    query_gain_any,
    key_gain_any,
    frequency_any,
    w_query_any,
    w_key_any,
    w_value_any,
    cache_keys_any,
    cache_values_any,
    w_out_any,
    own_out,
    send_out,
    lengths,
    requests,
    hidden,
    attn_gain,
    query_gain,
    key_gain,
    frequency,
    w_query,
    w_key,
    w_value,
    cache_keys,
    cache_values,
    w_out,
    sems,
):
    copies = []

    def fetch(source, target, parts):
        rows = target.shape[0] // parts
        group = []
        for i in range(parts):
            copy = pltpu.make_async_copy(
                source.at[pl.ds(i * rows, rows)], target.at[pl.ds(i * rows, rows)], sems.at[len(copies)]
            )
            copy.start()
            copies.append(copy)
            group.append(copy)
        return group

    small_copies = fetch(hidden_any, hidden, 1) + fetch(requests_any, requests, 1)
    small_copies += fetch(lengths_any, lengths, 1) + fetch(frequency_any, frequency, 1)
    small_copies += fetch(attn_gain_any, attn_gain, 1) + fetch(query_gain_any, query_gain, 1)
    small_copies += fetch(key_gain_any, key_gain, 1)
    query_copies = fetch(w_query_any, w_query, QUERY_PARTS)
    key_copies = fetch(w_key_any, w_key, 2)
    value_copies = fetch(w_value_any, w_value, 2)
    cached_key_copies = fetch(cache_keys_any.at[0], cache_keys, CACHE_PARTS)
    cached_value_copies = fetch(cache_values_any.at[0], cache_values, CACHE_PARTS)
    out_copies = fetch(w_out_any, w_out, OUT_PARTS)

    row_count, width = hidden.shape
    query_heads = w_query.shape[1] // HEAD_DIM
    value_heads = w_key.shape[1] // HEAD_DIM
    group = query_heads // value_heads
    span = cache_keys.shape[0]
    for copy in small_copies:
        copy.wait()
    cache_len = lengths[requests[lax.axis_index("req")]]

    row = lax.broadcasted_iota(jnp.int32, (row_count, HEAD_DIM), 0)
    lane = lax.broadcasted_iota(jnp.int32, (row_count, HEAD_DIM), 1)
    angles = (row + cache_len).astype(jnp.float32) * frequency[...]
    cosine = jnp.cos(angles)
    sine = jnp.where(lane < HEAD_DIM // 2, -jnp.sin(angles), jnp.sin(angles))

    def turned(heads, gain):
        scale = lax.rsqrt(jnp.mean(heads * heads, axis=-1, keepdims=True) + EPS)
        heads = heads * scale * gain
        return (heads * cosine + pltpu.roll(heads, HEAD_DIM // 2, 1) * sine).astype(jnp.bfloat16)

    tokens = hidden[...].astype(jnp.float32)
    scale = lax.rsqrt(jnp.mean(tokens * tokens, axis=-1, keepdims=True) + EPS)
    normed = (tokens * scale * attn_gain[...]).astype(jnp.bfloat16)

    def project(weight, group_copies):
        rows = width // len(group_copies)
        total = None
        for i, copy in enumerate(group_copies):
            copy.wait()
            part = jnp.dot(
                normed[:, i * rows : (i + 1) * rows],
                weight[i * rows : (i + 1) * rows, :],
                preferred_element_type=jnp.float32,
            )
            total = part if total is None else total + part
        return total

    def head(field, h):
        return field[:, h * HEAD_DIM : (h + 1) * HEAD_DIM]

    projected = project(w_query, query_copies)
    queries = [turned(head(projected, h), query_gain[...]) for h in range(query_heads)]
    queries = [jnp.concatenate(queries[k * group : (k + 1) * group], axis=0) for k in range(value_heads)]
    projected = project(w_key, key_copies)
    keys_new = [turned(head(projected, k), key_gain[...]) for k in range(value_heads)]
    values_new = project(w_value, value_copies).astype(jnp.bfloat16)

    factor = HEAD_DIM**-0.5 * LOG2E
    contract = (((1,), (1,)), ((), ()))
    totals, blended = [], []
    query_row = lax.broadcasted_iota(jnp.int32, (group * row_count, row_count), 0) % row_count
    column = lax.broadcasted_iota(jnp.int32, (group * row_count, row_count), 1)
    causal = jnp.where(query_row >= column, -SHIFT, NEG)
    for k in range(value_heads):
        scores = lax.dot_general(queries[k], keys_new[k], contract, preferred_element_type=jnp.float32)
        weights = jnp.exp2(scores * factor + causal)
        totals.append(jnp.sum(weights, axis=-1, keepdims=True))
        blended.append(
            jnp.dot(weights.astype(jnp.bfloat16), head(values_new, k), preferred_element_type=jnp.float32)
        )
    rows = span // CACHE_PARTS
    place_in_cache = lax.broadcasted_iota(jnp.int32, (1, rows), 1)
    for i in range(CACHE_PARTS):
        cached_key_copies[i].wait()
        stored = jnp.where(place_in_cache + i * rows < cache_len, -SHIFT, NEG)
        part = []
        for k in range(value_heads):
            keys = cache_keys[i * rows : (i + 1) * rows, k * HEAD_DIM : (k + 1) * HEAD_DIM]
            scores = lax.dot_general(queries[k], keys, contract, preferred_element_type=jnp.float32)
            weights = jnp.exp2(scores * factor + stored)
            totals[k] = totals[k] + jnp.sum(weights, axis=-1, keepdims=True)
            part.append(weights.astype(jnp.bfloat16))
        cached_value_copies[i].wait()
        for k in range(value_heads):
            values = cache_values[i * rows : (i + 1) * rows, k * HEAD_DIM : (k + 1) * HEAD_DIM]
            blended[k] = blended[k] + jnp.dot(part[k], values, preferred_element_type=jnp.float32)
    attended = []
    for k in range(value_heads):
        result = (blended[k] / totals[k]).astype(jnp.bfloat16)
        attended += [result[g * row_count : (g + 1) * row_count] for g in range(group)]
    attended = jnp.concatenate(attended, axis=1)
    for copy in out_copies:
        copy.wait()
    projected = jnp.dot(attended, w_out[...], preferred_element_type=jnp.float32)
    own_out[...] = tokens + projected
    send_out[...] = projected.astype(jnp.bfloat16)


def attention_rows(
    hidden_in, attn_gain, w_query, w_key, w_value, query_gain, key_gain, w_out,
    cache_keys, cache_values, cache_lengths, slot_request,
):
    half = HEAD_DIM // 2
    frequency = ROPE_BASE ** (-2.0 * np.arange(half, dtype=np.float64) / HEAD_DIM)
    frequency = jnp.asarray(np.tile(frequency, 2)[None, :], jnp.float32)
    vmem = pl.BlockSpec(memory_space=pltpu.VMEM)
    anywhere = pl.BlockSpec(memory_space=pltpu.HBM)
    rows, width = hidden_in.shape
    return pl.pallas_call(
        attention_kernel,
        out_shape=(pltpu.VMEM((rows, width), jnp.float32), pltpu.VMEM((rows, width), jnp.bfloat16)),
        in_specs=[anywhere] * 13,
        out_specs=(vmem, vmem),
        scratch_shapes=[
            pltpu.SMEM(cache_lengths.shape, jnp.int32),
            pltpu.SMEM(slot_request.shape, jnp.int32),
            pltpu.VMEM(hidden_in.shape, jnp.bfloat16),
            pltpu.VMEM((1, width), jnp.float32),
            pltpu.VMEM((1, HEAD_DIM), jnp.float32),
            pltpu.VMEM((1, HEAD_DIM), jnp.float32),
            pltpu.VMEM((1, HEAD_DIM), jnp.float32),
            pltpu.VMEM(w_query.shape, jnp.bfloat16),
            pltpu.VMEM(w_key.shape, jnp.bfloat16),
            pltpu.VMEM(w_value.shape, jnp.bfloat16),
            pltpu.VMEM(cache_keys.shape[1:], jnp.bfloat16),
            pltpu.VMEM(cache_values.shape[1:], jnp.bfloat16),
            pltpu.VMEM(w_out.shape, jnp.bfloat16),
            pltpu.SemaphoreType.DMA((QUERY_PARTS + 11 + 2 * CACHE_PARTS + OUT_PARTS,)),
        ],
        compiler_params=pltpu.CompilerParams(vmem_limit_bytes=40 * 1024 * 1024),
        cost_estimate=pl.CostEstimate(flops=1400000000, bytes_accessed=17500000, transcendentals=1100000),
        name="attention_rows",
    )(*[
        pltpu.with_memory_space_constraint(operand, pltpu.HBM)
        for operand in (
            cache_lengths, slot_request, hidden_in, attn_gain[None, :], query_gain[None, :],
            key_gain[None, :], frequency, w_query, w_key, w_value, cache_keys, cache_values, w_out,
        )
    ])


def mix_rows(own, other, mlp_gain):
    rows, half = own.shape[0], mlp_gain.shape[1]

    def body(own, other, gain, mixed_out, residual_out):
        total = own[...] + other[...].astype(jnp.float32)
        scale = lax.rsqrt(jnp.mean(total * total, axis=1, keepdims=True) + EPS)
        for part in range(2):

            @pl.when(lax.axis_index("head") == part)
            def _():
                kept = total[:, part * half : (part + 1) * half]
                residual_out[...] = kept
                mixed_out[...] = (kept * scale * gain[...]).astype(jnp.bfloat16)

    outs = [((rows, half), jnp.bfloat16), ((rows, half), jnp.float32)]
    return kernel_call(body, outs, 1000000, "mix_rows", own, other, mlp_gain)


def stacked(blocks, name, gates=(), flops=1000000):
    rows, width = sum(block.shape[0] for block in blocks), blocks[0].shape[1]

    def body(*refs):
        start = 0
        for ref in refs[:-1]:
            refs[-1][start : start + ref.shape[0]] = ref[...]
            start += ref.shape[0]

    return kernel_call(body, [((rows, width), jnp.bfloat16)], flops, name, *blocks, gates=gates)[0]


def gate_up(blocks, w_gate, w_up, name, gates=()):
    rows, units = sum(block.shape[0] for block in blocks), w_gate.shape[1]

    def body(*refs):
        start = 0
        w_gate, w_up, own_out, send_out = refs[-4:]
        for ref in refs[:-4]:
            for i, weight in enumerate((w_gate, w_up)):
                part = jnp.dot(ref[...], weight[...], preferred_element_type=jnp.float32)
                own_out[i, start : start + ref.shape[0]] = part
                send_out[i, start : start + ref.shape[0]] = part.astype(jnp.bfloat16)
            start += ref.shape[0]

    outs = [((2, rows, units), jnp.float32), ((2, rows, units), jnp.bfloat16)]
    flops = 4 * rows * w_gate.size
    return kernel_call(body, outs, flops, name, *blocks, w_gate, w_up, gates=gates)


def down_parts(own, other, w_down, outs, name, gates=()):
    rows = own.shape[1]

    def body(own, other, w_down, *out_refs):
        gate = own[0] + other[0].astype(jnp.float32)
        up = own[1] + other[1].astype(jnp.float32)
        active = (gate / (1.0 + jnp.exp(-gate)) * up).astype(jnp.bfloat16)
        start = 0
        for ref in out_refs:
            stop = start + ref.shape[0]
            part = jnp.dot(active[start:stop], w_down[...], preferred_element_type=jnp.float32)
            ref[...] = part.astype(ref.dtype)
            start = stop

    return kernel_call(body, outs, 2 * rows * w_down.size, name, own, other, w_down, gates=gates)


def summed(terms, outs, name, gates=(), flops=1000000):
    def body(*refs):
        total = None
        for ref in refs[: len(terms)]:
            part = ref[...].astype(jnp.float32)
            total = part if total is None else total + part
        for ref, (start, shape, dtype) in zip(refs[len(terms) :], outs):
            ref[...] = total[start : start + shape[0]].astype(dtype)

    plain = [(shape, dtype) for _, shape, dtype in outs]
    return kernel_call(body, plain, flops, name, *terms, gates=gates)


def on_device(
    hidden_in,
    attn_gain,
    w_query,
    w_key,
    w_value,
    query_gain,
    key_gain,
    w_out,
    cache_keys,
    cache_values,
    cache_lengths,
    slot_request,
    mlp_gain,
    w_gate,
    w_up,
    w_down,
    final_gain,
    w_vocab,
):
    row_count = hidden_in.shape[0]
    half_width = mlp_gain.shape[0]
    count = lax.axis_size("req")
    own, sent = attention_rows(
        hidden_in, attn_gain, w_query, w_key, w_value, query_gain, key_gain, w_out,
        cache_keys, cache_values, cache_lengths, slot_request,
    )
    mixed, residual = mix_rows(own, other_core(sent), mlp_gain[None, :])
    shape = mixed.shape
    outer, middle, inner, diagonal = along(count, 0), along(count, 1), along(count, 2), across(count)

    columns = [send(mixed, count, steps) for steps in outer]
    corners = [send(mixed, count, steps) for steps in diagonal]
    column = stacked([mixed] + columns, "column", gates=corners)
    corner = stacked(corners, "corner") if len(corners) > 1 else corners[0] if corners else None
    far = [send(column, count, steps) for steps in inner + middle]
    far_corners = [send(corner, count, steps) for steps in outer] if corners else []

    near_own, near_sent = gate_up([column] + ([corner] if corners else []), w_gate, w_up, "near_gate_up")
    near_rows = near_own.shape[1]
    near_outs = [(column.shape, jnp.float32)] + ([(corner.shape, jnp.float32)] if corners else [])
    near = down_parts(near_own, other_core(near_sent), w_down, near_outs, "near_down")

    far_corner = []
    if corners:
        far_corner = [stacked(far_corners, "far_corner", gates=(near_own,), flops=WEIGHT)]
        far = lax.optimization_barrier((far, far_corner))[0]

    at_home = (0, 0, 0)
    places = [at_home] + outer + diagonal
    for steps in inner + middle:
        places += [add_steps(steps, line) for line in [at_home] + outer]
    for steps in outer if corners else []:
        places += [add_steps(steps, turn) for turn in diagonal]
    last_shape = (count, half_width)
    blocks = [column] + ([corner] if corners else []) + far + far_corner

    def request_of(steps, requests):
        slots = lax.broadcasted_iota(jnp.int32, (1, count), 1)
        slot = slot_behind(lax.axis_index("req"), count, steps)
        return jnp.sum(jnp.where(slots == slot, requests[...], 0), axis=1, keepdims=True)

    def last_gate_up(*refs):
        requests, w_gate, w_up, own_out, send_out = refs[-5:]
        order = lax.broadcasted_iota(jnp.int32, (count, 1), 0)
        rows, place = jnp.zeros(last_shape, jnp.float32), 0
        for ref in refs[:-5]:
            for stop in range(row_count, ref.shape[0] + 1, row_count):
                last = ref[stop - 16 : stop].astype(jnp.float32)[15:]
                rows = rows + jnp.where(order == request_of(places[place], requests), last, 0.0)
                place += 1
        rows = rows.astype(jnp.bfloat16)
        for i, weight in enumerate((w_gate, w_up)):
            part = jnp.dot(rows, weight[...], preferred_element_type=jnp.float32)
            own_out[i] = part
            send_out[i] = part.astype(jnp.bfloat16)

    units = w_gate.shape[1]
    last_own, last_sent = kernel_call(
        last_gate_up, [((2, count, units), jnp.float32), ((2, count, units), jnp.bfloat16)], 100000000,
        "last_gate_up", *blocks, slot_request[None, :], w_gate, w_up,
    )
    def last_down(own, other, w_down, residual, requests, kept_out, sent_out):
        gate = own[0] + other[0].astype(jnp.float32)
        up = own[1] + other[1].astype(jnp.float32)
        active = (gate / (1.0 + jnp.exp(-gate)) * up).astype(jnp.bfloat16)
        order = lax.broadcasted_iota(jnp.int32, (count, 1), 0)
        total = jnp.dot(active, w_down[...], preferred_element_type=jnp.float32)
        total = total + jnp.where(order == request_of(at_home, requests), residual[row_count - 1 :, :], 0.0)
        kept_out[...] = total
        sent_out[...] = total.astype(jnp.bfloat16)

    last_outs = [(last_shape, jnp.float32), (last_shape, jnp.bfloat16)]
    last_kept, last_sent = kernel_call(
        last_down, last_outs, 100000000, "last_down",
        last_own, other_core(last_sent), w_down, residual, slot_request[None, :],
    )
    far_own, far_sent = gate_up(far + far_corner, w_gate, w_up, "far_gate_up", gates=(near[0], last_kept))
    last_plane = [send(last_sent, count, steps) for steps in inner + middle + diagonal]
    last_outs = [(0, last_shape, jnp.float32), (0, last_shape, jnp.bfloat16)]
    far_outs = [(column.shape, jnp.bfloat16) for _ in far] + [(corner.shape, jnp.bfloat16) for _ in far_corners]
    parts = down_parts(far_own, other_core(far_sent), w_down, far_outs, "far_down")
    last_kept, last_sent = summed([last_kept] + last_plane, last_outs, "last_plane", gates=(parts[0],))
    last_lines = [send(last_sent, count, steps) for steps in outer]
    half_rows = summed([last_kept] + last_lines, [(0, last_shape, jnp.float32)], "last_line")[0]
    near_parts, far_parts = parts[: len(far)], parts[len(far) :]
    near_parts = lax.optimization_barrier((near_parts, last_kept))[0]
    half_rows, far_parts = lax.optimization_barrier((half_rows, far_parts))

    returned = [send(part, count, back(steps)) for part, steps in zip(near_parts, inner + middle)]
    returned_corners = [send(part, count, back(steps)) for part, steps in zip(far_parts, outer)]

    other_rows = other_core(half_rows)
    final_rows = jnp.where(
        lax.axis_index("head") == 0,
        jnp.concatenate([half_rows, other_rows], axis=1),
        jnp.concatenate([other_rows, half_rows], axis=1),
    )
    scale = lax.rsqrt(jnp.mean(final_rows * final_rows, axis=-1, keepdims=True) + EPS)
    final_rows = (final_rows * scale * final_gain).astype(jnp.bfloat16)
    logits = jnp.dot(final_rows, w_vocab, preferred_element_type=jnp.float32)
    own_max = jnp.max(logits, axis=1)
    own_total = jnp.sum(jnp.exp(logits - own_max[:, None]), axis=1)
    stats = jnp.zeros((8, 128), jnp.float32).at[0, :count].set(own_max).at[1, :count].set(own_total)
    corner_sent = []
    if corners:
        corner_outs = [(row_count * i, shape, jnp.bfloat16) for i in range(len(corners))]
        corner_pieces = summed([near[1]] + returned_corners, corner_outs, "corner_sum", flops=WEIGHT)
        corner_sent = [send(part, count, back(steps)) for part, steps in zip(corner_pieces, diagonal)]
        returned = lax.optimization_barrier((returned, corner_pieces))[0]

    column_outs = [(0, shape, jnp.float32)]
    column_outs += [(row_count * (i + 1), shape, jnp.bfloat16) for i in range(len(outer))]
    pieces = summed([near[0]] + returned, column_outs, "column_sum", gates=(stats,))
    final = [residual, pieces[0]] + corner_sent + [
        send(part, count, back(steps)) for part, steps in zip(pieces[1:], outer)
    ]
    hidden_out = final[0]
    for part in final[1:]:
        hidden_out = hidden_out + part.astype(jnp.float32)
    hidden_out = hidden_out.astype(jnp.bfloat16)
    everyone = to_all(lax.optimization_barrier((stats, pieces))[0], ("req", "head"))
    row_max = jnp.max(everyone[:, 0, :count], axis=0)
    row_total = jnp.sum(everyone[:, 1, :count] * jnp.exp(everyone[:, 0, :count] - row_max[None, :]), axis=0)
    log_probs = logits - (row_max + jnp.log(row_total))[:, None]

    return (hidden_out, log_probs)


def solution(mesh):
    in_specs = (
        P("req", None),
        P(),
        P(None, "head"),
        P(None, "head"),
        P(None, "head"),
        P(),
        P(),
        P("head", None),
        P("req", None, "head"),
        P("req", None, "head"),
        P(),
        P(),
        P("head"),
        P("head", "req"),
        P("head", "req"),
        P("req", "head"),
        P(),
        P(None, ("req", "head")),
    )
    out_specs = (P("req", "head"), P(None, ("req", "head")))
    return jax.shard_map(
        on_device, mesh=mesh, in_specs=in_specs, out_specs=out_specs, check_vma=False
    )
```

```python
import jax
import jax.numpy as jnp
import numpy as np
from jax import lax
from jax.experimental import pallas as pl
from jax.experimental.pallas import tpu as pltpu
from jax.sharding import PartitionSpec as P


HEAD_DIM = 128


EPS = 1e-06
ROPE_BASE = 1000000.0
NEG = -1e30
WEIGHT = 20000000000
VMEM_SPEC = pl.BlockSpec(memory_space=pltpu.VMEM)
LOG2E = 1.4426950408889634
SHIFT = 4.0
QUERY_PARTS, CACHE_PARTS, OUT_PARTS = 4, 4, 4


def sizes_of(count):
    if count == 16:
        return (4, 2, 2)
    side = round(count ** (1 / 3))
    if side**3 == count:
        return (side, side, side)
    return (count, 1, 1)


def send(rows, count, steps):
    sizes = sizes_of(count)
    pairs = []
    for i in range(count):
        target, left = 0, i
        places = []
        for size in reversed(sizes):
            places.append(left % size)
            left //= size
        for place, size, step in zip(reversed(places), sizes, steps):
            target = target * size + (place + step) % size
        pairs.append((i, target))
    return lax.ppermute(rows, "req", pairs)


def along(count, digit):
    steps = []
    for step in range(1, sizes_of(count)[digit]):
        one = [0, 0, 0]
        one[digit] = step
        steps.append(tuple(one))
    return steps


def across(count):
    return [(0, b[1], c[2]) for b in along(count, 1) for c in along(count, 2)]


def add_steps(one, two):
    return tuple(a + b for a, b in zip(one, two))


def slot_behind(slot, count, steps):
    result, stride = 0, 1
    for size, step in zip(reversed(sizes_of(count)), reversed(steps)):
        result = result + lax.rem(lax.div(slot, stride) + size - step % size, size) * stride
        stride *= size
    return result


def back(steps):
    return tuple(-step for step in steps)


def other_core(rows):
    return lax.ppermute(rows, "head", [(0, 1), (1, 0)])


def to_all(block, names):
    count = lax.axis_size(names)
    return lax.all_to_all(jnp.broadcast_to(block[None], (count,) + block.shape), names, 0, 0, tiled=True)


def kernel_call(body, outs, flops, name, *operands, gates=(), pinned=True):
    def run(*refs):
        body(*refs[: len(operands)], *refs[len(operands) + len(gates) :])

    result = pl.pallas_call(
        run,
        out_shape=tuple((pltpu.VMEM if pinned else jax.ShapeDtypeStruct)(shape, dtype) for shape, dtype in outs),
        in_specs=[VMEM_SPEC] * len(operands) + [pl.BlockSpec(memory_space=pl.ANY)] * len(gates),
        out_specs=(VMEM_SPEC,) * len(outs),
        compiler_params=pltpu.CompilerParams(vmem_limit_bytes=20 * 1024 * 1024),
        cost_estimate=pl.CostEstimate(flops=flops, bytes_accessed=1000000, transcendentals=0),
        name=name,
    )(*operands, *gates)
    return result


def attention_kernel(
    lengths_any,
    requests_any,
    hidden_any,
    attn_gain_any,
    query_gain_any,
    key_gain_any,
    frequency_any,
    w_query_any,
    w_key_any,
    w_value_any,
    cache_keys_any,
    cache_values_any,
    w_out_any,
    own_out,
    send_out,
    lengths,
    requests,
    hidden,
    attn_gain,
    query_gain,
    key_gain,
    frequency,
    w_query,
    w_key,
    w_value,
    cache_keys,
    cache_values,
    w_out,
    sems,
):
    copies = []

    def fetch(source, target, parts):
        rows = target.shape[0] // parts
        group = []
        for i in range(parts):
            copy = pltpu.make_async_copy(
                source.at[pl.ds(i * rows, rows)], target.at[pl.ds(i * rows, rows)], sems.at[len(copies)]
            )
            copy.start()
            copies.append(copy)
            group.append(copy)
        return group

    small_copies = fetch(hidden_any, hidden, 1) + fetch(requests_any, requests, 1)
    small_copies += fetch(lengths_any, lengths, 1) + fetch(frequency_any, frequency, 1)
    small_copies += fetch(attn_gain_any, attn_gain, 1) + fetch(query_gain_any, query_gain, 1)
    small_copies += fetch(key_gain_any, key_gain, 1)
    query_copies = fetch(w_query_any, w_query, QUERY_PARTS)
    key_copies = fetch(w_key_any, w_key, 2)
    value_copies = fetch(w_value_any, w_value, 2)
    cached_key_copies = fetch(cache_keys_any.at[0], cache_keys, CACHE_PARTS)
    cached_value_copies = fetch(cache_values_any.at[0], cache_values, CACHE_PARTS)
    out_copies = fetch(w_out_any, w_out, OUT_PARTS)

    row_count, width = hidden.shape
    query_heads = w_query.shape[1] // HEAD_DIM
    value_heads = w_key.shape[1] // HEAD_DIM
    group = query_heads // value_heads
    span = cache_keys.shape[0]
    for copy in small_copies:
        copy.wait()
    cache_len = lengths[requests[lax.axis_index("req")]]

    row = lax.broadcasted_iota(jnp.int32, (row_count, HEAD_DIM), 0)
    lane = lax.broadcasted_iota(jnp.int32, (row_count, HEAD_DIM), 1)
    angles = (row + cache_len).astype(jnp.float32) * frequency[...]
    cosine = jnp.cos(angles)
    sine = jnp.where(lane < HEAD_DIM // 2, -jnp.sin(angles), jnp.sin(angles))

    def turned(heads, gain):
        scale = lax.rsqrt(jnp.mean(heads * heads, axis=-1, keepdims=True) + EPS)
        heads = heads * scale * gain
        return (heads * cosine + pltpu.roll(heads, HEAD_DIM // 2, 1) * sine).astype(jnp.bfloat16)

    tokens = hidden[...].astype(jnp.float32)
    scale = lax.rsqrt(jnp.mean(tokens * tokens, axis=-1, keepdims=True) + EPS)
    normed = (tokens * scale * attn_gain[...]).astype(jnp.bfloat16)

    def project(weight, group_copies):
        rows = width // len(group_copies)
        total = None
        for i, copy in enumerate(group_copies):
            copy.wait()
            part = jnp.dot(
                normed[:, i * rows : (i + 1) * rows],
                weight[i * rows : (i + 1) * rows, :],
                preferred_element_type=jnp.float32,
            )
            total = part if total is None else total + part
        return total

    def head(field, h):
        return field[:, h * HEAD_DIM : (h + 1) * HEAD_DIM]

    projected = project(w_query, query_copies)
    queries = [turned(head(projected, h), query_gain[...]) for h in range(query_heads)]
    queries = [jnp.concatenate(queries[k * group : (k + 1) * group], axis=0) for k in range(value_heads)]
    projected = project(w_key, key_copies)
    keys_new = [turned(head(projected, k), key_gain[...]) for k in range(value_heads)]
    values_new = project(w_value, value_copies).astype(jnp.bfloat16)

    factor = HEAD_DIM**-0.5 * LOG2E
    contract = (((1,), (1,)), ((), ()))
    totals, blended = [], []
    query_row = lax.broadcasted_iota(jnp.int32, (group * row_count, row_count), 0) % row_count
    column = lax.broadcasted_iota(jnp.int32, (group * row_count, row_count), 1)
    causal = jnp.where(query_row >= column, -SHIFT, NEG)
    for k in range(value_heads):
        scores = lax.dot_general(queries[k], keys_new[k], contract, preferred_element_type=jnp.float32)
        weights = jnp.exp2(scores * factor + causal)
        totals.append(jnp.sum(weights, axis=-1, keepdims=True))
        blended.append(
            jnp.dot(weights.astype(jnp.bfloat16), head(values_new, k), preferred_element_type=jnp.float32)
        )
    rows = span // CACHE_PARTS
    place_in_cache = lax.broadcasted_iota(jnp.int32, (1, rows), 1)
    for i in range(CACHE_PARTS):
        cached_key_copies[i].wait()
        stored = jnp.where(place_in_cache + i * rows < cache_len, -SHIFT, NEG)
        part = []
        for k in range(value_heads):
            keys = cache_keys[i * rows : (i + 1) * rows, k * HEAD_DIM : (k + 1) * HEAD_DIM]
            scores = lax.dot_general(queries[k], keys, contract, preferred_element_type=jnp.float32)
            weights = jnp.exp2(scores * factor + stored)
            totals[k] = totals[k] + jnp.sum(weights, axis=-1, keepdims=True)
            part.append(weights.astype(jnp.bfloat16))
        cached_value_copies[i].wait()
        for k in range(value_heads):
            values = cache_values[i * rows : (i + 1) * rows, k * HEAD_DIM : (k + 1) * HEAD_DIM]
            blended[k] = blended[k] + jnp.dot(part[k], values, preferred_element_type=jnp.float32)
    attended = []
    for k in range(value_heads):
        result = (blended[k] / totals[k]).astype(jnp.bfloat16)
        attended += [result[g * row_count : (g + 1) * row_count] for g in range(group)]
    attended = jnp.concatenate(attended, axis=1)
    for copy in out_copies:
        copy.wait()
    projected = jnp.dot(attended, w_out[...], preferred_element_type=jnp.float32)
    own_out[...] = tokens + projected
    send_out[...] = projected.astype(jnp.bfloat16)


def attention_rows(
    hidden_in, attn_gain, w_query, w_key, w_value, query_gain, key_gain, w_out,
    cache_keys, cache_values, cache_lengths, slot_request,
):
    half = HEAD_DIM // 2
    frequency = ROPE_BASE ** (-2.0 * np.arange(half, dtype=np.float64) / HEAD_DIM)
    frequency = jnp.asarray(np.tile(frequency, 2)[None, :], jnp.float32)
    vmem = pl.BlockSpec(memory_space=pltpu.VMEM)
    anywhere = pl.BlockSpec(memory_space=pltpu.HBM)
    rows, width = hidden_in.shape
    return pl.pallas_call(
        attention_kernel,
        out_shape=(pltpu.VMEM((rows, width), jnp.float32), pltpu.VMEM((rows, width), jnp.bfloat16)),
        in_specs=[anywhere] * 13,
        out_specs=(vmem, vmem),
        scratch_shapes=[
            pltpu.SMEM(cache_lengths.shape, jnp.int32),
            pltpu.SMEM(slot_request.shape, jnp.int32),
            pltpu.VMEM(hidden_in.shape, jnp.bfloat16),
            pltpu.VMEM((1, width), jnp.float32),
            pltpu.VMEM((1, HEAD_DIM), jnp.float32),
            pltpu.VMEM((1, HEAD_DIM), jnp.float32),
            pltpu.VMEM((1, HEAD_DIM), jnp.float32),
            pltpu.VMEM(w_query.shape, jnp.bfloat16),
            pltpu.VMEM(w_key.shape, jnp.bfloat16),
            pltpu.VMEM(w_value.shape, jnp.bfloat16),
            pltpu.VMEM(cache_keys.shape[1:], jnp.bfloat16),
            pltpu.VMEM(cache_values.shape[1:], jnp.bfloat16),
            pltpu.VMEM(w_out.shape, jnp.bfloat16),
            pltpu.SemaphoreType.DMA((QUERY_PARTS + 11 + 2 * CACHE_PARTS + OUT_PARTS,)),
        ],
        compiler_params=pltpu.CompilerParams(vmem_limit_bytes=40 * 1024 * 1024),
        cost_estimate=pl.CostEstimate(flops=1400000000, bytes_accessed=17500000, transcendentals=1100000),
        name="attention_rows",
    )(*[
        pltpu.with_memory_space_constraint(operand, pltpu.HBM)
        for operand in (
            cache_lengths, slot_request, hidden_in, attn_gain[None, :], query_gain[None, :],
            key_gain[None, :], frequency, w_query, w_key, w_value, cache_keys, cache_values, w_out,
        )
    ])


def mix_rows(own, other, mlp_gain):
    rows, half = own.shape[0], mlp_gain.shape[1]

    def body(own, other, gain, mixed_out, residual_out):
        total = own[...] + other[...].astype(jnp.float32)
        scale = lax.rsqrt(jnp.mean(total * total, axis=1, keepdims=True) + EPS)
        for part in range(2):

            @pl.when(lax.axis_index("head") == part)
            def _():
                kept = total[:, part * half : (part + 1) * half]
                residual_out[...] = kept
                mixed_out[...] = (kept * scale * gain[...]).astype(jnp.bfloat16)

    outs = [((rows, half), jnp.bfloat16), ((rows, half), jnp.float32)]
    return kernel_call(body, outs, 1000000, "mix_rows", own, other, mlp_gain)


def stacked(blocks, name, gates=(), flops=1000000):
    rows, width = sum(block.shape[0] for block in blocks), blocks[0].shape[1]

    def body(*refs):
        start = 0
        for ref in refs[:-1]:
            refs[-1][start : start + ref.shape[0]] = ref[...]
            start += ref.shape[0]

    return kernel_call(body, [((rows, width), jnp.bfloat16)], flops, name, *blocks, gates=gates)[0]


def gate_up(blocks, w_gate, w_up, name, gates=()):
    rows, units = sum(block.shape[0] for block in blocks), w_gate.shape[1]

    def body(*refs):
        start = 0
        w_gate, w_up, own_out, send_out = refs[-4:]
        for ref in refs[:-4]:
            for i, weight in enumerate((w_gate, w_up)):
                part = jnp.dot(ref[...], weight[...], preferred_element_type=jnp.float32)
                own_out[i, start : start + ref.shape[0]] = part
                send_out[i, start : start + ref.shape[0]] = part.astype(jnp.bfloat16)
            start += ref.shape[0]

    outs = [((2, rows, units), jnp.float32), ((2, rows, units), jnp.bfloat16)]
    flops = 4 * rows * w_gate.size
    return kernel_call(body, outs, flops, name, *blocks, w_gate, w_up, gates=gates)


def down_parts(own, other, w_down, outs, name, gates=()):
    rows = own.shape[1]

    def body(own, other, w_down, *out_refs):
        gate = own[0] + other[0].astype(jnp.float32)
        up = own[1] + other[1].astype(jnp.float32)
        active = (gate / (1.0 + jnp.exp(-gate)) * up).astype(jnp.bfloat16)
        start = 0
        for ref in out_refs:
            stop = start + ref.shape[0]
            part = jnp.dot(active[start:stop], w_down[...], preferred_element_type=jnp.float32)
            ref[...] = part.astype(ref.dtype)
            start = stop

    return kernel_call(body, outs, 2 * rows * w_down.size, name, own, other, w_down, gates=gates)


def summed(terms, outs, name, gates=(), flops=1000000, pinned=True):
    def body(*refs):
        total = None
        for ref in refs[: len(terms)]:
            part = ref[...].astype(jnp.float32)
            total = part if total is None else total + part
        for ref, (start, shape, dtype) in zip(refs[len(terms) :], outs):
            ref[...] = total[start : start + shape[0]].astype(dtype)

    plain = [(shape, dtype) for _, shape, dtype in outs]
    return kernel_call(body, plain, flops, name, *terms, gates=gates, pinned=pinned)


def on_device(
    hidden_in,
    attn_gain,
    w_query,
    w_key,
    w_value,
    query_gain,
    key_gain,
    w_out,
    cache_keys,
    cache_values,
    cache_lengths,
    slot_request,
    mlp_gain,
    w_gate,
    w_up,
    w_down,
    final_gain,
    w_vocab,
):
    row_count = hidden_in.shape[0]
    half_width = mlp_gain.shape[0]
    count = lax.axis_size("req")
    own, sent = attention_rows(
        hidden_in, attn_gain, w_query, w_key, w_value, query_gain, key_gain, w_out,
        cache_keys, cache_values, cache_lengths, slot_request,
    )
    mixed, residual = mix_rows(own, other_core(sent), mlp_gain[None, :])
    shape = mixed.shape
    outer, middle, inner, diagonal = along(count, 0), along(count, 1), along(count, 2), across(count)

    columns = [send(mixed, count, steps) for steps in outer]
    corners = [send(mixed, count, steps) for steps in diagonal]
    column = stacked([mixed] + columns, "column", gates=corners)
    corner = stacked(corners, "corner") if len(corners) > 1 else corners[0] if corners else None
    far = [send(column, count, steps) for steps in inner + middle]
    far_corners = [send(corner, count, steps) for steps in outer] if corners else []

    near_own, near_sent = gate_up([column] + ([corner] if corners else []), w_gate, w_up, "near_gate_up")
    near_rows = near_own.shape[1]
    near_outs = [(column.shape, jnp.float32)] + ([(corner.shape, jnp.float32)] if corners else [])
    near = down_parts(near_own, other_core(near_sent), w_down, near_outs, "near_down")

    far_corner = []
    if corners:
        far_corner = [stacked(far_corners, "far_corner", gates=(near_own,), flops=WEIGHT)]
        far = lax.optimization_barrier((far, far_corner))[0]

    at_home = (0, 0, 0)
    places = [at_home] + outer + diagonal
    for steps in inner + middle:
        places += [add_steps(steps, line) for line in [at_home] + outer]
    for steps in outer if corners else []:
        places += [add_steps(steps, turn) for turn in diagonal]
    last_shape = (count, half_width)
    blocks = [column] + ([corner] if corners else []) + far + far_corner

    def request_of(steps, requests):
        slots = lax.broadcasted_iota(jnp.int32, (1, count), 1)
        slot = slot_behind(lax.axis_index("req"), count, steps)
        return jnp.sum(jnp.where(slots == slot, requests[...], 0), axis=1, keepdims=True)

    def last_gate_up(*refs):
        requests, w_gate, w_up, own_out, send_out = refs[-5:]
        order = lax.broadcasted_iota(jnp.int32, (count, 1), 0)
        rows, place = jnp.zeros(last_shape, jnp.float32), 0
        for ref in refs[:-5]:
            for stop in range(row_count, ref.shape[0] + 1, row_count):
                last = ref[stop - 16 : stop].astype(jnp.float32)[15:]
                rows = rows + jnp.where(order == request_of(places[place], requests), last, 0.0)
                place += 1
        rows = rows.astype(jnp.bfloat16)
        for i, weight in enumerate((w_gate, w_up)):
            part = jnp.dot(rows, weight[...], preferred_element_type=jnp.float32)
            own_out[i] = part
            send_out[i] = part.astype(jnp.bfloat16)

    units = w_gate.shape[1]
    last_own, last_sent = kernel_call(
        last_gate_up, [((2, count, units), jnp.float32), ((2, count, units), jnp.bfloat16)], 100000000,
        "last_gate_up", *blocks, slot_request[None, :], w_gate, w_up,
    )
    def last_down(own, other, w_down, residual, requests, kept_out, sent_out):
        gate = own[0] + other[0].astype(jnp.float32)
        up = own[1] + other[1].astype(jnp.float32)
        active = (gate / (1.0 + jnp.exp(-gate)) * up).astype(jnp.bfloat16)
        order = lax.broadcasted_iota(jnp.int32, (count, 1), 0)
        total = jnp.dot(active, w_down[...], preferred_element_type=jnp.float32)
        total = total + jnp.where(order == request_of(at_home, requests), residual[row_count - 1 :, :], 0.0)
        kept_out[...] = total
        sent_out[...] = total.astype(jnp.bfloat16)

    last_outs = [(last_shape, jnp.float32), (last_shape, jnp.bfloat16)]
    last_kept, last_sent = kernel_call(
        last_down, last_outs, 100000000, "last_down",
        last_own, other_core(last_sent), w_down, residual, slot_request[None, :],
    )
    far_own, far_sent = gate_up(far + far_corner, w_gate, w_up, "far_gate_up", gates=(near[0], last_kept))
    last_lines = [send(last_sent, count, steps) for steps in outer]
    last_outs = [(0, last_shape, jnp.float32), (0, last_shape, jnp.bfloat16)]
    far_outs = [(column.shape, jnp.bfloat16) for _ in far] + [(corner.shape, jnp.bfloat16) for _ in far_corners]
    parts = down_parts(far_own, other_core(far_sent), w_down, far_outs, "far_down")
    last_outs = [(0, last_shape, jnp.float32), (0, last_shape, jnp.bfloat16)]

    def join_lines(*refs):
        lines, sources = refs[1 : 1 + len(outer)], refs[1 + len(outer) : 1 + len(outer) + len(far)]
        kept_out, sent_out, *packed_outs = refs[1 + len(outer) + len(far) :]
        total = refs[0][...]
        for ref in lines:
            total = total + ref[...].astype(jnp.float32)
        kept_out[...] = total
        sent_out[...] = total.astype(jnp.bfloat16)
        for source, ref in zip(sources, packed_outs):
            ref[: source.shape[0]] = source[...]
            ref[source.shape[0] :] = total.astype(jnp.bfloat16)

    column_rows = column.shape[0]
    packed_out = ((column_rows + count, half_width), jnp.bfloat16)
    last_kept, last_sent, *packed = kernel_call(
        join_lines, [(last_shape, jnp.float32), (last_shape, jnp.bfloat16)] + [packed_out] * len(far), 1000000,
        "join_lines", last_kept, *last_lines, *parts[: len(far)],
    )

    returned = [send(part, count, back(steps)) for part, steps in zip(packed, inner + middle)]
    last_corners = [send(last_sent, count, steps) for steps in diagonal]
    far_parts = lax.optimization_barrier((parts[len(far) :], last_kept))[0]
    returned_corners = [send(part, count, back(steps)) for part, steps in zip(far_parts, outer)]

    def join_columns(*refs):
        own, last, sums = refs[0], refs[1], refs[2 : 2 + len(far)]
        turns, out_refs = refs[2 + len(far) : 2 + len(far) + len(diagonal)], refs[2 + len(far) + len(diagonal) :]
        for i, ref in enumerate(out_refs[:-1]):
            rows = slice(i * row_count, (i + 1) * row_count)
            total = own[rows]
            for part in sums:
                total = total + part[rows].astype(jnp.float32)
            ref[...] = total.astype(ref.dtype)
        total = last[...]
        for part in sums:
            total = total + part[column_rows:].astype(jnp.float32)
        for part in turns:
            total = total + part[...].astype(jnp.float32)
        out_refs[-1][...] = total

    column_outs = [(shape, jnp.float32)] + [(shape, jnp.bfloat16)] * len(outer) + [(last_shape, jnp.float32)]
    *pieces, half_rows = kernel_call(
        join_columns, column_outs, 1000000, "join_columns", near[0], last_kept, *returned, *last_corners,
    )
    devices = count * lax.axis_size("head")
    vocab = w_vocab.shape[1]

    def vocab_logits(own, other, gain, weight, logits_out, stats_out):
        rows = []
        for part in range(2):
            mine = lax.axis_index("head") == part
            rows.append(jnp.where(mine, own[...], other[...]))
        rows = jnp.concatenate(rows, axis=1)
        scale = lax.rsqrt(jnp.mean(rows * rows, axis=1, keepdims=True) + EPS)
        rows = (rows * scale * gain[...]).astype(jnp.bfloat16)
        largest = None
        for start in range(0, vocab, 512):
            stop = min(start + 512, vocab)
            part = lax.dot_general(
                rows, weight[start:stop, :], (((1,), (1,)), ((), ())), preferred_element_type=jnp.float32
            )
            logits_out[:, start:stop] = part
            top = jnp.max(part, axis=1, keepdims=True)
            largest = top if largest is None else jnp.maximum(largest, top)
        total = jnp.sum(jnp.exp(logits_out[...] - largest), axis=1, keepdims=True)
        row = lax.broadcasted_iota(jnp.int32, (count, 128), 0)
        lane = lax.broadcasted_iota(jnp.int32, (count, 128), 1)
        stats = jnp.where(lane == row, largest, 0.0) + jnp.where(lane == row + 64, total, 0.0)
        stats_out[...] = jnp.broadcast_to(jnp.sum(stats, axis=0)[None, None], stats_out.shape)

    logits, stats = kernel_call(
        vocab_logits, [((count, vocab), jnp.float32), ((devices, 1, 128), jnp.float32)], 2 * count * w_vocab.size,
        "vocab_logits", half_rows, other_core(half_rows), final_gain[None, :],
        pltpu.with_memory_space_constraint(w_vocab.T, pltpu.VMEM),
    )
    corner_sent = []
    if corners:
        corner_outs = [(row_count * i, shape, jnp.bfloat16) for i in range(len(corners))]
        corner_pieces = summed([near[1]] + returned_corners, corner_outs, "corner_sum", gates=(stats,))
        corner_sent = [send(part, count, back(steps)) for part, steps in zip(corner_pieces, diagonal)]
    final = [residual, pieces[0]] + corner_sent + [
        send(part, count, back(steps)) for part, steps in zip(pieces[1:], outer)
    ]
    everyone = lax.all_to_all(stats, ("req", "head"), 0, 0, tiled=True)

    def finish(*refs):
        logits, everyone, hidden_out, log_out = *refs[:2], *refs[-2:]
        total = None
        for ref in refs[2:-2]:
            part = ref[...].astype(jnp.float32)
            total = part if total is None else total + part
        hidden_out[...] = total.astype(jnp.bfloat16)
        tiles = everyone[...]
        top = jnp.max(tiles, axis=0, keepdims=True)
        scaled = jnp.exp(jnp.minimum(tiles - top, 0.0))[:, :64] * tiles[:, 64:]
        shift = top[:, :64] + jnp.log(jnp.sum(scaled, axis=0, keepdims=True))
        row = lax.broadcasted_iota(jnp.int32, (count, 64), 0)
        lane = lax.broadcasted_iota(jnp.int32, (count, 64), 1)
        log_out[...] = logits[...] - jnp.sum(jnp.where(lane == row, shift, 0.0), axis=1, keepdims=True)

    outs = [(shape, jnp.bfloat16), ((count, vocab), jnp.float32)]
    return kernel_call(finish, outs, WEIGHT, "finish", logits, everyone[:, 0], *final, pinned=False)


def solution(mesh):
    in_specs = (
        P("req", None),
        P(),
        P(None, "head"),
        P(None, "head"),
        P(None, "head"),
        P(),
        P(),
        P("head", None),
        P("req", None, "head"),
        P("req", None, "head"),
        P(),
        P(),
        P("head"),
        P("head", "req"),
        P("head", "req"),
        P("req", "head"),
        P(),
        P(None, ("req", "head")),
    )
    out_specs = (P("req", "head"), P(None, ("req", "head")))
    return jax.shard_map(
        on_device, mesh=mesh, in_specs=in_specs, out_specs=out_specs, check_vma=False
    )
```

```python
import jax
import jax.numpy as jnp
import numpy as np
from jax import lax
from jax.experimental import pallas as pl
from jax.experimental.pallas import tpu as pltpu
from jax.sharding import PartitionSpec as P


HEAD_DIM = 128


EPS = 1e-06
ROPE_BASE = 1000000.0
NEG = -1e30
WEIGHT = 20000000000
VMEM_SPEC = pl.BlockSpec(memory_space=pltpu.VMEM)
LOG2E = 1.4426950408889634
SHIFT = 4.0
QUERY_PARTS, CACHE_PARTS, OUT_PARTS = 4, 4, 4


def sizes_of(count):
    if count == 16:
        return (4, 2, 2)
    side = round(count ** (1 / 3))
    if side**3 == count:
        return (side, side, side)
    return (count, 1, 1)


def moved(place, size, step):
    if size & (size - 1) == 0:
        return place ^ abs(step)
    return (place + step) % size


def send(rows, count, steps):
    sizes = sizes_of(count)
    pairs = []
    for i in range(count):
        target, left = 0, i
        places = []
        for size in reversed(sizes):
            places.append(left % size)
            left //= size
        for place, size, step in zip(reversed(places), sizes, steps):
            target = target * size + moved(place, size, step)
        pairs.append((i, target))
    return lax.ppermute(rows, "req", pairs)


def along(count, digit):
    steps = []
    for step in reversed(range(1, sizes_of(count)[digit])):
        one = [0, 0, 0]
        one[digit] = step
        steps.append(tuple(one))
    return steps


def across(count):
    return [(0, b[1], c[2]) for b in along(count, 1) for c in along(count, 2)]


def add_steps(one, two):
    return tuple(a + b for a, b in zip(one, two))


def slot_behind(slot, count, steps):
    result, stride = 0, 1
    for size, step in zip(reversed(sizes_of(count)), reversed(steps)):
        place = lax.rem(lax.div(slot, stride), size)
        if size & (size - 1) == 0:
            place = place ^ abs(step)
        else:
            place = lax.rem(place + size - step % size, size)
        result = result + place * stride
        stride *= size
    return result


def back(steps):
    return tuple(-step for step in steps)


def other_core(rows):
    return lax.ppermute(rows, "head", [(0, 1), (1, 0)])


def to_all(block, names):
    count = lax.axis_size(names)
    return lax.all_to_all(jnp.broadcast_to(block[None], (count,) + block.shape), names, 0, 0, tiled=True)


def kernel_call(body, outs, flops, name, *operands, gates=(), pinned=True):
    def run(*refs):
        body(*refs[: len(operands)], *refs[len(operands) + len(gates) :])

    result = pl.pallas_call(
        run,
        out_shape=tuple((pltpu.VMEM if pinned else jax.ShapeDtypeStruct)(shape, dtype) for shape, dtype in outs),
        in_specs=[VMEM_SPEC] * len(operands) + [pl.BlockSpec(memory_space=pl.ANY)] * len(gates),
        out_specs=(VMEM_SPEC,) * len(outs),
        compiler_params=pltpu.CompilerParams(vmem_limit_bytes=20 * 1024 * 1024),
        cost_estimate=pl.CostEstimate(flops=flops, bytes_accessed=1000000, transcendentals=0),
        name=name,
    )(*operands, *gates)
    return result


def attention_kernel(
    lengths_any,
    requests_any,
    hidden_any,
    attn_gain_any,
    query_gain_any,
    key_gain_any,
    frequency_any,
    w_query_any,
    w_key_any,
    w_value_any,
    cache_keys_any,
    cache_values_any,
    w_out_any,
    own_out,
    send_out,
    lengths,
    requests,
    hidden,
    attn_gain,
    query_gain,
    key_gain,
    frequency,
    w_query,
    w_key,
    w_value,
    cache_keys,
    cache_values,
    w_out,
    sems,
):
    copies = []

    def fetch(source, target, parts):
        rows = target.shape[0] // parts
        group = []
        for i in range(parts):
            copy = pltpu.make_async_copy(
                source.at[pl.ds(i * rows, rows)], target.at[pl.ds(i * rows, rows)], sems.at[len(copies)]
            )
            copy.start()
            copies.append(copy)
            group.append(copy)
        return group

    small_copies = fetch(hidden_any, hidden, 1) + fetch(requests_any, requests, 1)
    small_copies += fetch(lengths_any, lengths, 1) + fetch(frequency_any, frequency, 1)
    small_copies += fetch(attn_gain_any, attn_gain, 1) + fetch(query_gain_any, query_gain, 1)
    small_copies += fetch(key_gain_any, key_gain, 1)
    query_copies = fetch(w_query_any, w_query, QUERY_PARTS)
    key_copies = fetch(w_key_any, w_key, 2)
    value_copies = fetch(w_value_any, w_value, 2)
    cached_key_copies = fetch(cache_keys_any.at[0], cache_keys, CACHE_PARTS)
    cached_value_copies = fetch(cache_values_any.at[0], cache_values, CACHE_PARTS)
    out_copies = fetch(w_out_any, w_out, OUT_PARTS)

    row_count, width = hidden.shape
    query_heads = w_query.shape[1] // HEAD_DIM
    value_heads = w_key.shape[1] // HEAD_DIM
    group = query_heads // value_heads
    span = cache_keys.shape[0]
    for copy in small_copies:
        copy.wait()
    cache_len = lengths[requests[lax.axis_index("req")]]

    row = lax.broadcasted_iota(jnp.int32, (row_count, HEAD_DIM), 0)
    lane = lax.broadcasted_iota(jnp.int32, (row_count, HEAD_DIM), 1)
    angles = (row + cache_len).astype(jnp.float32) * frequency[...]
    cosine = jnp.cos(angles)
    sine = jnp.where(lane < HEAD_DIM // 2, -jnp.sin(angles), jnp.sin(angles))

    def turned(heads, gain):
        scale = lax.rsqrt(jnp.mean(heads * heads, axis=-1, keepdims=True) + EPS)
        heads = heads * scale * gain
        return (heads * cosine + pltpu.roll(heads, HEAD_DIM // 2, 1) * sine).astype(jnp.bfloat16)

    tokens = hidden[...].astype(jnp.float32)
    scale = lax.rsqrt(jnp.mean(tokens * tokens, axis=-1, keepdims=True) + EPS)
    normed = (tokens * scale * attn_gain[...]).astype(jnp.bfloat16)

    def project(weight, group_copies):
        rows = width // len(group_copies)
        total = None
        for i, copy in enumerate(group_copies):
            copy.wait()
            part = jnp.dot(
                normed[:, i * rows : (i + 1) * rows],
                weight[i * rows : (i + 1) * rows, :],
                preferred_element_type=jnp.float32,
            )
            total = part if total is None else total + part
        return total

    def head(field, h):
        return field[:, h * HEAD_DIM : (h + 1) * HEAD_DIM]

    projected = project(w_query, query_copies)
    queries = [turned(head(projected, h), query_gain[...]) for h in range(query_heads)]
    queries = [jnp.concatenate(queries[k * group : (k + 1) * group], axis=0) for k in range(value_heads)]
    projected = project(w_key, key_copies)
    keys_new = [turned(head(projected, k), key_gain[...]) for k in range(value_heads)]
    values_new = project(w_value, value_copies).astype(jnp.bfloat16)

    factor = HEAD_DIM**-0.5 * LOG2E
    contract = (((1,), (1,)), ((), ()))
    totals, blended = [], []
    query_row = lax.broadcasted_iota(jnp.int32, (group * row_count, row_count), 0) % row_count
    column = lax.broadcasted_iota(jnp.int32, (group * row_count, row_count), 1)
    causal = jnp.where(query_row >= column, -SHIFT, NEG)
    for k in range(value_heads):
        scores = lax.dot_general(queries[k], keys_new[k], contract, preferred_element_type=jnp.float32)
        weights = jnp.exp2(scores * factor + causal)
        totals.append(jnp.sum(weights, axis=-1, keepdims=True))
        blended.append(
            jnp.dot(weights.astype(jnp.bfloat16), head(values_new, k), preferred_element_type=jnp.float32)
        )
    rows = span // CACHE_PARTS
    place_in_cache = lax.broadcasted_iota(jnp.int32, (1, rows), 1)
    for i in range(CACHE_PARTS):
        cached_key_copies[i].wait()
        stored = jnp.where(place_in_cache + i * rows < cache_len, -SHIFT, NEG)
        part = []
        for k in range(value_heads):
            keys = cache_keys[i * rows : (i + 1) * rows, k * HEAD_DIM : (k + 1) * HEAD_DIM]
            scores = lax.dot_general(queries[k], keys, contract, preferred_element_type=jnp.float32)
            weights = jnp.exp2(scores * factor + stored)
            totals[k] = totals[k] + jnp.sum(weights, axis=-1, keepdims=True)
            part.append(weights.astype(jnp.bfloat16))
        cached_value_copies[i].wait()
        for k in range(value_heads):
            values = cache_values[i * rows : (i + 1) * rows, k * HEAD_DIM : (k + 1) * HEAD_DIM]
            blended[k] = blended[k] + jnp.dot(part[k], values, preferred_element_type=jnp.float32)
    attended = []
    for k in range(value_heads):
        result = (blended[k] / totals[k]).astype(jnp.bfloat16)
        attended += [result[g * row_count : (g + 1) * row_count] for g in range(group)]
    attended = jnp.concatenate(attended, axis=1)
    for copy in out_copies:
        copy.wait()
    projected = jnp.dot(attended, w_out[...], preferred_element_type=jnp.float32)
    own_out[...] = tokens + projected
    send_out[...] = projected.astype(jnp.bfloat16)


def attention_rows(
    hidden_in, attn_gain, w_query, w_key, w_value, query_gain, key_gain, w_out,
    cache_keys, cache_values, cache_lengths, slot_request,
):
    half = HEAD_DIM // 2
    frequency = ROPE_BASE ** (-2.0 * np.arange(half, dtype=np.float64) / HEAD_DIM)
    frequency = jnp.asarray(np.tile(frequency, 2)[None, :], jnp.float32)
    vmem = pl.BlockSpec(memory_space=pltpu.VMEM)
    anywhere = pl.BlockSpec(memory_space=pltpu.HBM)
    rows, width = hidden_in.shape
    return pl.pallas_call(
        attention_kernel,
        out_shape=(pltpu.VMEM((rows, width), jnp.float32), pltpu.VMEM((rows, width), jnp.bfloat16)),
        in_specs=[anywhere] * 13,
        out_specs=(vmem, vmem),
        scratch_shapes=[
            pltpu.SMEM(cache_lengths.shape, jnp.int32),
            pltpu.SMEM(slot_request.shape, jnp.int32),
            pltpu.VMEM(hidden_in.shape, jnp.bfloat16),
            pltpu.VMEM((1, width), jnp.float32),
            pltpu.VMEM((1, HEAD_DIM), jnp.float32),
            pltpu.VMEM((1, HEAD_DIM), jnp.float32),
            pltpu.VMEM((1, HEAD_DIM), jnp.float32),
            pltpu.VMEM(w_query.shape, jnp.bfloat16),
            pltpu.VMEM(w_key.shape, jnp.bfloat16),
            pltpu.VMEM(w_value.shape, jnp.bfloat16),
            pltpu.VMEM(cache_keys.shape[1:], jnp.bfloat16),
            pltpu.VMEM(cache_values.shape[1:], jnp.bfloat16),
            pltpu.VMEM(w_out.shape, jnp.bfloat16),
            pltpu.SemaphoreType.DMA((QUERY_PARTS + 11 + 2 * CACHE_PARTS + OUT_PARTS,)),
        ],
        compiler_params=pltpu.CompilerParams(vmem_limit_bytes=40 * 1024 * 1024),
        cost_estimate=pl.CostEstimate(flops=1400000000, bytes_accessed=17500000, transcendentals=1100000),
        name="attention_rows",
    )(*[
        pltpu.with_memory_space_constraint(operand, pltpu.HBM)
        for operand in (
            cache_lengths, slot_request, hidden_in, attn_gain[None, :], query_gain[None, :],
            key_gain[None, :], frequency, w_query, w_key, w_value, cache_keys, cache_values, w_out,
        )
    ])


def mix_rows(own, other, mlp_gain):
    rows, half = own.shape[0], mlp_gain.shape[1]

    def body(own, other, gain, mixed_out, residual_out):
        total = own[...] + other[...].astype(jnp.float32)
        scale = lax.rsqrt(jnp.mean(total * total, axis=1, keepdims=True) + EPS)
        for part in range(2):

            @pl.when(lax.axis_index("head") == part)
            def _():
                kept = total[:, part * half : (part + 1) * half]
                residual_out[...] = kept
                mixed_out[...] = (kept * scale * gain[...]).astype(jnp.bfloat16)

    outs = [((rows, half), jnp.bfloat16), ((rows, half), jnp.float32)]
    return kernel_call(body, outs, 1000000, "mix_rows", own, other, mlp_gain)


def stacked(blocks, name, gates=(), flops=1000000):
    rows, width = sum(block.shape[0] for block in blocks), blocks[0].shape[1]

    def body(*refs):
        start = 0
        for ref in refs[:-1]:
            refs[-1][start : start + ref.shape[0]] = ref[...]
            start += ref.shape[0]

    return kernel_call(body, [((rows, width), jnp.bfloat16)], flops, name, *blocks, gates=gates)[0]


def gate_up(blocks, w_gate, w_up, name, gates=()):
    rows, units = sum(block.shape[0] for block in blocks), w_gate.shape[1]

    def body(*refs):
        start = 0
        w_gate, w_up, own_out, send_out = refs[-4:]
        for ref in refs[:-4]:
            for i, weight in enumerate((w_gate, w_up)):
                part = jnp.dot(ref[...], weight[...], preferred_element_type=jnp.float32)
                own_out[i, start : start + ref.shape[0]] = part
                send_out[i, start : start + ref.shape[0]] = part.astype(jnp.bfloat16)
            start += ref.shape[0]

    outs = [((2, rows, units), jnp.float32), ((2, rows, units), jnp.bfloat16)]
    flops = 4 * rows * w_gate.size
    return kernel_call(body, outs, flops, name, *blocks, w_gate, w_up, gates=gates)


def down_parts(own, other, w_down, outs, name, gates=()):
    rows = own.shape[1]

    def body(own, other, w_down, *out_refs):
        gate = own[0] + other[0].astype(jnp.float32)
        up = own[1] + other[1].astype(jnp.float32)
        active = (gate / (1.0 + jnp.exp(-gate)) * up).astype(jnp.bfloat16)
        start = 0
        for ref in out_refs:
            stop = start + ref.shape[0]
            part = jnp.dot(active[start:stop], w_down[...], preferred_element_type=jnp.float32)
            ref[...] = part.astype(ref.dtype)
            start = stop

    return kernel_call(body, outs, 2 * rows * w_down.size, name, own, other, w_down, gates=gates)


def summed(terms, outs, name, gates=(), flops=1000000, pinned=True):
    def body(*refs):
        total = None
        for ref in refs[: len(terms)]:
            part = ref[...].astype(jnp.float32)
            total = part if total is None else total + part
        for ref, (start, shape, dtype) in zip(refs[len(terms) :], outs):
            ref[...] = total[start : start + shape[0]].astype(dtype)

    plain = [(shape, dtype) for _, shape, dtype in outs]
    return kernel_call(body, plain, flops, name, *terms, gates=gates, pinned=pinned)


def on_device(
    hidden_in,
    attn_gain,
    w_query,
    w_key,
    w_value,
    query_gain,
    key_gain,
    w_out,
    cache_keys,
    cache_values,
    cache_lengths,
    slot_request,
    mlp_gain,
    w_gate,
    w_up,
    w_down,
    final_gain,
    w_vocab,
):
    row_count = hidden_in.shape[0]
    half_width = mlp_gain.shape[0]
    count = lax.axis_size("req")
    own, sent = attention_rows(
        hidden_in, attn_gain, w_query, w_key, w_value, query_gain, key_gain, w_out,
        cache_keys, cache_values, cache_lengths, slot_request,
    )
    mixed, residual = mix_rows(own, other_core(sent), mlp_gain[None, :])
    shape = mixed.shape
    outer, middle, inner, diagonal = along(count, 0), along(count, 1), along(count, 2), across(count)

    columns = [send(mixed, count, steps) for steps in outer]
    corners = [send(mixed, count, steps) for steps in diagonal]
    column = stacked([mixed] + columns, "column", gates=corners)
    corner = stacked(corners, "corner") if len(corners) > 1 else corners[0] if corners else None
    far = [send(column, count, steps) for steps in inner + middle]
    far_corners = [send(corner, count, steps) for steps in outer] if corners else []

    near_own, near_sent = gate_up([column] + ([corner] if corners else []), w_gate, w_up, "near_gate_up")
    near_rows = near_own.shape[1]
    near_outs = [(column.shape, jnp.float32)] + ([(corner.shape, jnp.float32)] if corners else [])
    near = down_parts(near_own, other_core(near_sent), w_down, near_outs, "near_down")

    far_corner = []
    if corners:
        far_corner = [stacked(far_corners, "far_corner", gates=(near_own,), flops=WEIGHT)]
        far = lax.optimization_barrier((far, far_corner))[0]

    at_home = (0, 0, 0)
    places = [at_home] + outer + diagonal
    for steps in inner + middle:
        places += [add_steps(steps, line) for line in [at_home] + outer]
    for steps in outer if corners else []:
        places += [add_steps(steps, turn) for turn in diagonal]
    last_shape = (count, half_width)
    blocks = [column] + ([corner] if corners else []) + far + far_corner

    def request_of(steps, requests):
        slots = lax.broadcasted_iota(jnp.int32, (1, count), 1)
        slot = slot_behind(lax.axis_index("req"), count, steps)
        return jnp.sum(jnp.where(slots == slot, requests[...], 0), axis=1, keepdims=True)

    def last_gate_up(*refs):
        requests, w_gate, w_up, own_out, send_out = refs[-5:]
        order = lax.broadcasted_iota(jnp.int32, (count, 1), 0)
        rows, place = jnp.zeros(last_shape, jnp.float32), 0
        for ref in refs[:-5]:
            for stop in range(row_count, ref.shape[0] + 1, row_count):
                last = ref[stop - 16 : stop].astype(jnp.float32)[15:]
                rows = rows + jnp.where(order == request_of(places[place], requests), last, 0.0)
                place += 1
        rows = rows.astype(jnp.bfloat16)
        for i, weight in enumerate((w_gate, w_up)):
            part = jnp.dot(rows, weight[...], preferred_element_type=jnp.float32)
            own_out[i] = part
            send_out[i] = part.astype(jnp.bfloat16)

    units = w_gate.shape[1]
    last_own, last_sent = kernel_call(
        last_gate_up, [((2, count, units), jnp.float32), ((2, count, units), jnp.bfloat16)], 100000000,
        "last_gate_up", *blocks, slot_request[None, :], w_gate, w_up,
    )
    def last_down(own, other, w_down, residual, requests, kept_out, sent_out):
        gate = own[0] + other[0].astype(jnp.float32)
        up = own[1] + other[1].astype(jnp.float32)
        active = (gate / (1.0 + jnp.exp(-gate)) * up).astype(jnp.bfloat16)
        order = lax.broadcasted_iota(jnp.int32, (count, 1), 0)
        total = jnp.dot(active, w_down[...], preferred_element_type=jnp.float32)
        total = total + jnp.where(order == request_of(at_home, requests), residual[row_count - 1 :, :], 0.0)
        kept_out[...] = total
        sent_out[...] = total.astype(jnp.bfloat16)

    last_outs = [(last_shape, jnp.float32), (last_shape, jnp.bfloat16)]
    last_kept, last_sent = kernel_call(
        last_down, last_outs, 100000000, "last_down",
        last_own, other_core(last_sent), w_down, residual, slot_request[None, :],
    )
    far_own, far_sent = gate_up(far + far_corner, w_gate, w_up, "far_gate_up", gates=(near[0], last_kept))
    last_lines = [send(last_sent, count, steps) for steps in outer]
    last_outs = [(0, last_shape, jnp.float32), (0, last_shape, jnp.bfloat16)]
    far_outs = [(column.shape, jnp.bfloat16) for _ in far] + [(corner.shape, jnp.bfloat16) for _ in far_corners]
    parts = down_parts(far_own, other_core(far_sent), w_down, far_outs, "far_down")
    last_outs = [(0, last_shape, jnp.float32), (0, last_shape, jnp.bfloat16)]

    def join_lines(*refs):
        lines, sources = refs[1 : 1 + len(outer)], refs[1 + len(outer) : 1 + len(outer) + len(far)]
        kept_out, sent_out, *packed_outs = refs[1 + len(outer) + len(far) :]
        total = refs[0][...]
        for ref in lines:
            total = total + ref[...].astype(jnp.float32)
        kept_out[...] = total
        sent_out[...] = total.astype(jnp.bfloat16)
        for source, ref in zip(sources, packed_outs):
            ref[: source.shape[0]] = source[...]
            ref[source.shape[0] :] = total.astype(jnp.bfloat16)

    column_rows = column.shape[0]
    packed_out = ((column_rows + count, half_width), jnp.bfloat16)
    last_kept, last_sent, *packed = kernel_call(
        join_lines, [(last_shape, jnp.float32), (last_shape, jnp.bfloat16)] + [packed_out] * len(far), 1000000,
        "join_lines", last_kept, *last_lines, *parts[: len(far)],
    )

    returned = [send(part, count, back(steps)) for part, steps in zip(packed, inner + middle)]
    last_corners = [send(last_sent, count, steps) for steps in diagonal]
    far_parts = lax.optimization_barrier((parts[len(far) :], last_kept))[0]
    returned_corners = [send(part, count, back(steps)) for part, steps in zip(far_parts, outer)]

    def join_columns(*refs):
        own, last, sums = refs[0], refs[1], refs[2 : 2 + len(far)]
        turns, out_refs = refs[2 + len(far) : 2 + len(far) + len(diagonal)], refs[2 + len(far) + len(diagonal) :]
        for i, ref in enumerate(out_refs[:-1]):
            rows = slice(i * row_count, (i + 1) * row_count)
            total = own[rows]
            for part in sums:
                total = total + part[rows].astype(jnp.float32)
            ref[...] = total.astype(ref.dtype)
        total = last[...]
        for part in sums:
            total = total + part[column_rows:].astype(jnp.float32)
        for part in turns:
            total = total + part[...].astype(jnp.float32)
        out_refs[-1][...] = total

    column_outs = [(shape, jnp.float32)] + [(shape, jnp.bfloat16)] * len(outer) + [(last_shape, jnp.float32)]
    *pieces, half_rows = kernel_call(
        join_columns, column_outs, 1000000, "join_columns", near[0], last_kept, *returned, *last_corners,
    )
    devices = count * lax.axis_size("head")
    vocab = w_vocab.shape[1]

    def vocab_logits(own, other, gain, weight, logits_out, stats_out):
        rows = []
        for part in range(2):
            mine = lax.axis_index("head") == part
            rows.append(jnp.where(mine, own[...], other[...]))
        rows = jnp.concatenate(rows, axis=1)
        scale = lax.rsqrt(jnp.mean(rows * rows, axis=1, keepdims=True) + EPS)
        rows = (rows * scale * gain[...]).astype(jnp.bfloat16)
        largest = None
        for start in range(0, vocab, 512):
            stop = min(start + 512, vocab)
            part = lax.dot_general(
                rows, weight[start:stop, :], (((1,), (1,)), ((), ())), preferred_element_type=jnp.float32
            )
            logits_out[:, start:stop] = part
            top = jnp.max(part, axis=1, keepdims=True)
            largest = top if largest is None else jnp.maximum(largest, top)
        total = jnp.sum(jnp.exp(logits_out[...] - largest), axis=1, keepdims=True)
        row = lax.broadcasted_iota(jnp.int32, (count, 128), 0)
        lane = lax.broadcasted_iota(jnp.int32, (count, 128), 1)
        stats = jnp.where(lane == row, largest, 0.0) + jnp.where(lane == row + 64, total, 0.0)
        stats_out[...] = jnp.broadcast_to(jnp.sum(stats, axis=0)[None, None], stats_out.shape)

    logits, stats = kernel_call(
        vocab_logits, [((count, vocab), jnp.float32), ((devices, 1, 128), jnp.float32)], 2 * count * w_vocab.size,
        "vocab_logits", half_rows, other_core(half_rows), final_gain[None, :],
        pltpu.with_memory_space_constraint(w_vocab.T, pltpu.VMEM),
    )
    corner_sent = []
    if corners:
        corner_outs = [(row_count * i, shape, jnp.bfloat16) for i in range(len(corners))]
        corner_pieces = summed([near[1]] + returned_corners, corner_outs, "corner_sum", gates=(stats,))
        corner_sent = [send(part, count, back(steps)) for part, steps in zip(corner_pieces, diagonal)]
    final = [residual, pieces[0]] + corner_sent + [
        send(part, count, back(steps)) for part, steps in zip(pieces[1:], outer)
    ]
    everyone = lax.all_to_all(stats, ("req", "head"), 0, 0, tiled=True)

    def finish(*refs):
        logits, everyone, hidden_out, log_out = *refs[:2], *refs[-2:]
        total = None
        for ref in refs[2:-2]:
            part = ref[...].astype(jnp.float32)
            total = part if total is None else total + part
        hidden_out[...] = total.astype(jnp.bfloat16)
        tiles = everyone[...]
        top = jnp.max(tiles, axis=0, keepdims=True)
        scaled = jnp.exp(jnp.minimum(tiles - top, 0.0))[:, :64] * tiles[:, 64:]
        shift = top[:, :64] + jnp.log(jnp.sum(scaled, axis=0, keepdims=True))
        row = lax.broadcasted_iota(jnp.int32, (count, 64), 0)
        lane = lax.broadcasted_iota(jnp.int32, (count, 64), 1)
        log_out[...] = logits[...] - jnp.sum(jnp.where(lane == row, shift, 0.0), axis=1, keepdims=True)

    outs = [(shape, jnp.bfloat16), ((count, vocab), jnp.float32)]
    return kernel_call(finish, outs, WEIGHT, "finish", logits, everyone[:, 0], *final, pinned=False)


def solution(mesh):
    in_specs = (
        P("req", None),
        P(),
        P(None, "head"),
        P(None, "head"),
        P(None, "head"),
        P(),
        P(),
        P("head", None),
        P("req", None, "head"),
        P("req", None, "head"),
        P(),
        P(),
        P("head"),
        P("head", "req"),
        P("head", "req"),
        P("req", "head"),
        P(),
        P(None, ("req", "head")),
    )
    out_specs = (P("req", "head"), P(None, ("req", "head")))
    return jax.shard_map(
        on_device, mesh=mesh, in_specs=in_specs, out_specs=out_specs, check_vma=False
    )
```

```python
import jax
import jax.numpy as jnp
import numpy as np
from jax import lax
from jax.experimental import pallas as pl
from jax.experimental.pallas import tpu as pltpu
from jax.sharding import PartitionSpec as P


HEAD_DIM = 128


EPS = 1e-06
ROPE_BASE = 1000000.0
NEG = -1e30
WEIGHT = 20000000000
VMEM_SPEC = pl.BlockSpec(memory_space=pltpu.VMEM)
LOG2E = 1.4426950408889634
SHIFT = 4.0
QUERY_PARTS, CACHE_PARTS, OUT_PARTS = 4, 1, 4


def sizes_of(count):
    if count == 16:
        return (4, 2, 2)
    side = round(count ** (1 / 3))
    if side**3 == count:
        return (side, side, side)
    return (count, 1, 1)


def moved(place, size, step):
    if size & (size - 1) == 0:
        return place ^ abs(step)
    return (place + step) % size


def send(rows, count, steps):
    sizes = sizes_of(count)
    pairs = []
    for i in range(count):
        target, left = 0, i
        places = []
        for size in reversed(sizes):
            places.append(left % size)
            left //= size
        for place, size, step in zip(reversed(places), sizes, steps):
            target = target * size + moved(place, size, step)
        pairs.append((i, target))
    return lax.ppermute(rows, "req", pairs)


def along(count, digit):
    steps = []
    for step in reversed(range(1, sizes_of(count)[digit])):
        one = [0, 0, 0]
        one[digit] = step
        steps.append(tuple(one))
    return steps


def across(count):
    return [(0, b[1], c[2]) for b in along(count, 1) for c in along(count, 2)]


def add_steps(one, two):
    return tuple(a + b for a, b in zip(one, two))


def slot_behind(slot, count, steps):
    result, stride = 0, 1
    for size, step in zip(reversed(sizes_of(count)), reversed(steps)):
        place = lax.rem(lax.div(slot, stride), size)
        if size & (size - 1) == 0:
            place = place ^ abs(step)
        else:
            place = lax.rem(place + size - step % size, size)
        result = result + place * stride
        stride *= size
    return result


def back(steps):
    return tuple(-step for step in steps)


def other_core(rows):
    return lax.ppermute(rows, "head", [(0, 1), (1, 0)])


def to_all(block, names):
    count = lax.axis_size(names)
    return lax.all_to_all(jnp.broadcast_to(block[None], (count,) + block.shape), names, 0, 0, tiled=True)


def kernel_call(body, outs, flops, name, *operands, gates=(), pinned=True):
    def run(*refs):
        body(*refs[: len(operands)], *refs[len(operands) + len(gates) :])

    result = pl.pallas_call(
        run,
        out_shape=tuple((pltpu.VMEM if pinned else jax.ShapeDtypeStruct)(shape, dtype) for shape, dtype in outs),
        in_specs=[VMEM_SPEC] * len(operands) + [pl.BlockSpec(memory_space=pl.ANY)] * len(gates),
        out_specs=(VMEM_SPEC,) * len(outs),
        compiler_params=pltpu.CompilerParams(vmem_limit_bytes=20 * 1024 * 1024),
        cost_estimate=pl.CostEstimate(flops=flops, bytes_accessed=1000000, transcendentals=0),
        name=name,
    )(*operands, *gates)
    return result


def attention_kernel(
    lengths_any,
    requests_any,
    hidden_any,
    attn_gain_any,
    query_gain_any,
    key_gain_any,
    frequency_any,
    w_query_any,
    w_key_any,
    w_value_any,
    cache_keys_any,
    cache_values_any,
    w_out_any,
    own_out,
    send_out,
    lengths,
    requests,
    hidden,
    attn_gain,
    query_gain,
    key_gain,
    frequency,
    w_query,
    w_key,
    w_value,
    cache_keys,
    cache_values,
    w_out,
    sems,
):
    copies = []

    def fetch(source, target, parts):
        rows = target.shape[0] // parts
        group = []
        for i in range(parts):
            copy = pltpu.make_async_copy(
                source.at[pl.ds(i * rows, rows)], target.at[pl.ds(i * rows, rows)], sems.at[len(copies)]
            )
            copy.start()
            copies.append(copy)
            group.append(copy)
        return group

    small_copies = fetch(hidden_any, hidden, 1) + fetch(requests_any, requests, 1)
    small_copies += fetch(lengths_any, lengths, 1) + fetch(frequency_any, frequency, 1)
    small_copies += fetch(attn_gain_any, attn_gain, 1) + fetch(query_gain_any, query_gain, 1)
    small_copies += fetch(key_gain_any, key_gain, 1)
    query_copies = fetch(w_query_any, w_query, QUERY_PARTS)
    key_copies = fetch(w_key_any, w_key, 2)
    value_copies = fetch(w_value_any, w_value, 2)
    cached_key_copies = fetch(cache_keys_any.at[0], cache_keys, CACHE_PARTS)
    cached_value_copies = fetch(cache_values_any.at[0], cache_values, CACHE_PARTS)
    out_copies = fetch(w_out_any, w_out, OUT_PARTS)

    row_count, width = hidden.shape
    query_heads = w_query.shape[1] // HEAD_DIM
    value_heads = w_key.shape[1] // HEAD_DIM
    group = query_heads // value_heads
    span = cache_keys.shape[0]
    for copy in small_copies:
        copy.wait()
    cache_len = lengths[requests[lax.axis_index("req")]]

    row = lax.broadcasted_iota(jnp.int32, (row_count, HEAD_DIM), 0)
    lane = lax.broadcasted_iota(jnp.int32, (row_count, HEAD_DIM), 1)
    angles = (row + cache_len).astype(jnp.float32) * frequency[...]
    cosine = jnp.cos(angles)
    sine = jnp.where(lane < HEAD_DIM // 2, -jnp.sin(angles), jnp.sin(angles))

    def turned(heads, gain):
        scale = lax.rsqrt(jnp.mean(heads * heads, axis=-1, keepdims=True) + EPS)
        heads = heads * scale * gain
        return (heads * cosine + pltpu.roll(heads, HEAD_DIM // 2, 1) * sine).astype(jnp.bfloat16)

    tokens = hidden[...].astype(jnp.float32)
    scale = lax.rsqrt(jnp.mean(tokens * tokens, axis=-1, keepdims=True) + EPS)
    normed = (tokens * scale * attn_gain[...]).astype(jnp.bfloat16)

    def project(weight, group_copies):
        rows = width // len(group_copies)
        total = None
        for i, copy in enumerate(group_copies):
            copy.wait()
            part = jnp.dot(
                normed[:, i * rows : (i + 1) * rows],
                weight[i * rows : (i + 1) * rows, :],
                preferred_element_type=jnp.float32,
            )
            total = part if total is None else total + part
        return total

    def head(field, h):
        return field[:, h * HEAD_DIM : (h + 1) * HEAD_DIM]

    projected = project(w_query, query_copies)
    queries = [turned(head(projected, h), query_gain[...]) for h in range(query_heads)]
    queries = [jnp.concatenate(queries[k * group : (k + 1) * group], axis=0) for k in range(value_heads)]
    projected = project(w_key, key_copies)
    keys_new = [turned(head(projected, k), key_gain[...]) for k in range(value_heads)]
    values_new = project(w_value, value_copies).astype(jnp.bfloat16)

    factor = HEAD_DIM**-0.5 * LOG2E
    contract = (((1,), (1,)), ((), ()))
    totals, blended = [], []
    query_row = lax.broadcasted_iota(jnp.int32, (group * row_count, row_count), 0) % row_count
    column = lax.broadcasted_iota(jnp.int32, (group * row_count, row_count), 1)
    causal = jnp.where(query_row >= column, -SHIFT, NEG)
    for k in range(value_heads):
        scores = lax.dot_general(queries[k], keys_new[k], contract, preferred_element_type=jnp.float32)
        weights = jnp.exp2(scores * factor + causal)
        totals.append(jnp.sum(weights, axis=-1, keepdims=True))
        blended.append(
            jnp.dot(weights.astype(jnp.bfloat16), head(values_new, k), preferred_element_type=jnp.float32)
        )
    rows = span // CACHE_PARTS
    place_in_cache = lax.broadcasted_iota(jnp.int32, (1, rows), 1)
    for i in range(CACHE_PARTS):
        cached_key_copies[i].wait()
        stored = jnp.where(place_in_cache + i * rows < cache_len, -SHIFT, NEG)
        part = []
        for k in range(value_heads):
            keys = cache_keys[i * rows : (i + 1) * rows, k * HEAD_DIM : (k + 1) * HEAD_DIM]
            scores = lax.dot_general(queries[k], keys, contract, preferred_element_type=jnp.float32)
            weights = jnp.exp2(scores * factor + stored)
            totals[k] = totals[k] + jnp.sum(weights, axis=-1, keepdims=True)
            part.append(weights.astype(jnp.bfloat16))
        cached_value_copies[i].wait()
        for k in range(value_heads):
            values = cache_values[i * rows : (i + 1) * rows, k * HEAD_DIM : (k + 1) * HEAD_DIM]
            blended[k] = blended[k] + jnp.dot(part[k], values, preferred_element_type=jnp.float32)
    attended = []
    for k in range(value_heads):
        result = (blended[k] / totals[k]).astype(jnp.bfloat16)
        attended += [result[g * row_count : (g + 1) * row_count] for g in range(group)]
    attended = jnp.concatenate(attended, axis=1)
    for copy in out_copies:
        copy.wait()
    projected = jnp.dot(attended, w_out[...], preferred_element_type=jnp.float32)
    own_out[...] = tokens + projected
    send_out[...] = projected.astype(jnp.bfloat16)


def attention_rows(
    hidden_in, attn_gain, w_query, w_key, w_value, query_gain, key_gain, w_out,
    cache_keys, cache_values, cache_lengths, slot_request,
):
    half = HEAD_DIM // 2
    frequency = ROPE_BASE ** (-2.0 * np.arange(half, dtype=np.float64) / HEAD_DIM)
    frequency = jnp.asarray(np.tile(frequency, 2)[None, :], jnp.float32)
    vmem = pl.BlockSpec(memory_space=pltpu.VMEM)
    anywhere = pl.BlockSpec(memory_space=pltpu.HBM)
    rows, width = hidden_in.shape
    return pl.pallas_call(
        attention_kernel,
        out_shape=(pltpu.VMEM((rows, width), jnp.float32), pltpu.VMEM((rows, width), jnp.bfloat16)),
        in_specs=[anywhere] * 13,
        out_specs=(vmem, vmem),
        scratch_shapes=[
            pltpu.SMEM(cache_lengths.shape, jnp.int32),
            pltpu.SMEM(slot_request.shape, jnp.int32),
            pltpu.VMEM(hidden_in.shape, jnp.bfloat16),
            pltpu.VMEM((1, width), jnp.float32),
            pltpu.VMEM((1, HEAD_DIM), jnp.float32),
            pltpu.VMEM((1, HEAD_DIM), jnp.float32),
            pltpu.VMEM((1, HEAD_DIM), jnp.float32),
            pltpu.VMEM(w_query.shape, jnp.bfloat16),
            pltpu.VMEM(w_key.shape, jnp.bfloat16),
            pltpu.VMEM(w_value.shape, jnp.bfloat16),
            pltpu.VMEM(cache_keys.shape[1:], jnp.bfloat16),
            pltpu.VMEM(cache_values.shape[1:], jnp.bfloat16),
            pltpu.VMEM(w_out.shape, jnp.bfloat16),
            pltpu.SemaphoreType.DMA((QUERY_PARTS + 11 + 2 * CACHE_PARTS + OUT_PARTS,)),
        ],
        compiler_params=pltpu.CompilerParams(vmem_limit_bytes=40 * 1024 * 1024),
        cost_estimate=pl.CostEstimate(flops=1400000000, bytes_accessed=17500000, transcendentals=1100000),
        name="attention_rows",
    )(*[
        pltpu.with_memory_space_constraint(operand, pltpu.HBM)
        for operand in (
            cache_lengths, slot_request, hidden_in, attn_gain[None, :], query_gain[None, :],
            key_gain[None, :], frequency, w_query, w_key, w_value, cache_keys, cache_values, w_out,
        )
    ])


def mix_rows(own, other, mlp_gain):
    rows, half = own.shape[0], mlp_gain.shape[1]

    def body(own, other, gain, mixed_out, residual_out):
        total = own[...] + other[...].astype(jnp.float32)
        scale = lax.rsqrt(jnp.mean(total * total, axis=1, keepdims=True) + EPS)
        for part in range(2):

            @pl.when(lax.axis_index("head") == part)
            def _():
                kept = total[:, part * half : (part + 1) * half]
                residual_out[...] = kept
                mixed_out[...] = (kept * scale * gain[...]).astype(jnp.bfloat16)

    outs = [((rows, half), jnp.bfloat16), ((rows, half), jnp.float32)]
    return kernel_call(body, outs, 1000000, "mix_rows", own, other, mlp_gain)


def stacked(blocks, name, gates=(), flops=1000000):
    rows, width = sum(block.shape[0] for block in blocks), blocks[0].shape[1]

    def body(*refs):
        start = 0
        for ref in refs[:-1]:
            refs[-1][start : start + ref.shape[0]] = ref[...]
            start += ref.shape[0]

    return kernel_call(body, [((rows, width), jnp.bfloat16)], flops, name, *blocks, gates=gates)[0]


def gate_up(blocks, w_gate, w_up, name, gates=()):
    rows, units = sum(block.shape[0] for block in blocks), w_gate.shape[1]

    def body(*refs):
        start = 0
        w_gate, w_up, own_out, send_out = refs[-4:]
        for ref in refs[:-4]:
            for i, weight in enumerate((w_gate, w_up)):
                part = jnp.dot(ref[...], weight[...], preferred_element_type=jnp.float32)
                own_out[i, start : start + ref.shape[0]] = part
                send_out[i, start : start + ref.shape[0]] = part.astype(jnp.bfloat16)
            start += ref.shape[0]

    outs = [((2, rows, units), jnp.float32), ((2, rows, units), jnp.bfloat16)]
    flops = 4 * rows * w_gate.size
    return kernel_call(body, outs, flops, name, *blocks, w_gate, w_up, gates=gates)


def down_parts(own, other, w_down, outs, name, gates=()):
    rows = own.shape[1]

    def body(own, other, w_down, *out_refs):
        gate = own[0] + other[0].astype(jnp.float32)
        up = own[1] + other[1].astype(jnp.float32)
        active = (gate / (1.0 + jnp.exp(-gate)) * up).astype(jnp.bfloat16)
        start = 0
        for ref in out_refs:
            stop = start + ref.shape[0]
            part = jnp.dot(active[start:stop], w_down[...], preferred_element_type=jnp.float32)
            ref[...] = part.astype(ref.dtype)
            start = stop

    return kernel_call(body, outs, 2 * rows * w_down.size, name, own, other, w_down, gates=gates)


def summed(terms, outs, name, gates=(), flops=1000000, pinned=True):
    def body(*refs):
        total = None
        for ref in refs[: len(terms)]:
            part = ref[...].astype(jnp.float32)
            total = part if total is None else total + part
        for ref, (start, shape, dtype) in zip(refs[len(terms) :], outs):
            ref[...] = total[start : start + shape[0]].astype(dtype)

    plain = [(shape, dtype) for _, shape, dtype in outs]
    return kernel_call(body, plain, flops, name, *terms, gates=gates, pinned=pinned)


def on_device(
    hidden_in,
    attn_gain,
    w_query,
    w_key,
    w_value,
    query_gain,
    key_gain,
    w_out,
    cache_keys,
    cache_values,
    cache_lengths,
    slot_request,
    mlp_gain,
    w_gate,
    w_up,
    w_down,
    final_gain,
    w_vocab,
):
    row_count = hidden_in.shape[0]
    half_width = mlp_gain.shape[0]
    count = lax.axis_size("req")
    own, sent = attention_rows(
        hidden_in, attn_gain, w_query, w_key, w_value, query_gain, key_gain, w_out,
        cache_keys, cache_values, cache_lengths, slot_request,
    )
    mixed, residual = mix_rows(own, other_core(sent), mlp_gain[None, :])
    shape = mixed.shape
    outer, middle, inner, diagonal = along(count, 0), along(count, 1), along(count, 2), across(count)

    columns = [send(mixed, count, steps) for steps in outer]
    corners = [send(mixed, count, steps) for steps in diagonal]
    column = stacked([mixed] + columns, "column", gates=corners)
    corner = stacked(corners, "corner") if len(corners) > 1 else corners[0] if corners else None
    far = [send(column, count, steps) for steps in inner + middle]
    far_corners = [send(corner, count, steps) for steps in outer] if corners else []

    near_own, near_sent = gate_up([column] + ([corner] if corners else []), w_gate, w_up, "near_gate_up")
    near_rows = near_own.shape[1]
    near_outs = [(column.shape, jnp.float32)] + ([(corner.shape, jnp.float32)] if corners else [])
    near = down_parts(near_own, other_core(near_sent), w_down, near_outs, "near_down")

    far_corner = []
    if corners:
        far_corner = [stacked(far_corners, "far_corner", gates=(near_own,), flops=WEIGHT)]
        far = lax.optimization_barrier((far, far_corner))[0]

    at_home = (0, 0, 0)
    places = [at_home] + outer + diagonal
    for steps in inner + middle:
        places += [add_steps(steps, line) for line in [at_home] + outer]
    for steps in outer if corners else []:
        places += [add_steps(steps, turn) for turn in diagonal]
    last_shape = (count, half_width)
    blocks = [column] + ([corner] if corners else []) + far + far_corner

    def request_of(steps, requests):
        slots = lax.broadcasted_iota(jnp.int32, (1, count), 1)
        slot = slot_behind(lax.axis_index("req"), count, steps)
        return jnp.sum(jnp.where(slots == slot, requests[...], 0), axis=1, keepdims=True)

    def last_gate_up(*refs):
        requests, w_gate, w_up, own_out, send_out = refs[-5:]
        order = lax.broadcasted_iota(jnp.int32, (count, 1), 0)
        rows, place = jnp.zeros(last_shape, jnp.float32), 0
        for ref in refs[:-5]:
            for stop in range(row_count, ref.shape[0] + 1, row_count):
                last = ref[stop - 16 : stop].astype(jnp.float32)[15:]
                rows = rows + jnp.where(order == request_of(places[place], requests), last, 0.0)
                place += 1
        rows = rows.astype(jnp.bfloat16)
        for i, weight in enumerate((w_gate, w_up)):
            part = jnp.dot(rows, weight[...], preferred_element_type=jnp.float32)
            own_out[i] = part
            send_out[i] = part.astype(jnp.bfloat16)

    units = w_gate.shape[1]
    last_own, last_sent = kernel_call(
        last_gate_up, [((2, count, units), jnp.float32), ((2, count, units), jnp.bfloat16)], 100000000,
        "last_gate_up", *blocks, slot_request[None, :], w_gate, w_up,
    )
    def last_down(own, other, w_down, residual, requests, kept_out, sent_out):
        gate = own[0] + other[0].astype(jnp.float32)
        up = own[1] + other[1].astype(jnp.float32)
        active = (gate / (1.0 + jnp.exp(-gate)) * up).astype(jnp.bfloat16)
        order = lax.broadcasted_iota(jnp.int32, (count, 1), 0)
        total = jnp.dot(active, w_down[...], preferred_element_type=jnp.float32)
        total = total + jnp.where(order == request_of(at_home, requests), residual[row_count - 1 :, :], 0.0)
        kept_out[...] = total
        sent_out[...] = total.astype(jnp.bfloat16)

    last_outs = [(last_shape, jnp.float32), (last_shape, jnp.bfloat16)]
    last_kept, last_sent = kernel_call(
        last_down, last_outs, 100000000, "last_down",
        last_own, other_core(last_sent), w_down, residual, slot_request[None, :],
    )
    far_own, far_sent = gate_up(far + far_corner, w_gate, w_up, "far_gate_up", gates=(near[0], last_kept))
    last_lines = [send(last_sent, count, steps) for steps in outer]
    last_outs = [(0, last_shape, jnp.float32), (0, last_shape, jnp.bfloat16)]
    far_outs = [(column.shape, jnp.bfloat16) for _ in far] + [(corner.shape, jnp.bfloat16) for _ in far_corners]
    parts = down_parts(far_own, other_core(far_sent), w_down, far_outs, "far_down")
    last_outs = [(0, last_shape, jnp.float32), (0, last_shape, jnp.bfloat16)]

    def join_lines(*refs):
        lines, sources = refs[1 : 1 + len(outer)], refs[1 + len(outer) : 1 + len(outer) + len(far)]
        kept_out, sent_out, *packed_outs = refs[1 + len(outer) + len(far) :]
        total = refs[0][...]
        for ref in lines:
            total = total + ref[...].astype(jnp.float32)
        kept_out[...] = total
        sent_out[...] = total.astype(jnp.bfloat16)
        for source, ref in zip(sources, packed_outs):
            ref[: source.shape[0]] = source[...]
            ref[source.shape[0] :] = total.astype(jnp.bfloat16)

    column_rows = column.shape[0]
    packed_out = ((column_rows + count, half_width), jnp.bfloat16)
    last_kept, last_sent, *packed = kernel_call(
        join_lines, [(last_shape, jnp.float32), (last_shape, jnp.bfloat16)] + [packed_out] * len(far), 1000000,
        "join_lines", last_kept, *last_lines, *parts[: len(far)],
    )

    returned = [send(part, count, back(steps)) for part, steps in zip(packed, inner + middle)]
    last_corners = [send(last_sent, count, steps) for steps in diagonal]
    far_parts = lax.optimization_barrier((parts[len(far) :], last_kept))[0]
    returned_corners = [send(part, count, back(steps)) for part, steps in zip(far_parts, outer)]

    def join_columns(*refs):
        own, last, sums = refs[0], refs[1], refs[2 : 2 + len(far)]
        turns, out_refs = refs[2 + len(far) : 2 + len(far) + len(diagonal)], refs[2 + len(far) + len(diagonal) :]
        for i, ref in enumerate(out_refs[:-1]):
            rows = slice(i * row_count, (i + 1) * row_count)
            total = own[rows]
            for part in sums:
                total = total + part[rows].astype(jnp.float32)
            ref[...] = total.astype(ref.dtype)
        total = last[...]
        for part in sums:
            total = total + part[column_rows:].astype(jnp.float32)
        for part in turns:
            total = total + part[...].astype(jnp.float32)
        out_refs[-1][...] = total

    column_outs = [(shape, jnp.float32)] + [(shape, jnp.bfloat16)] * len(outer) + [(last_shape, jnp.float32)]
    *pieces, half_rows = kernel_call(
        join_columns, column_outs, 1000000, "join_columns", near[0], last_kept, *returned, *last_corners,
    )
    devices = count * lax.axis_size("head")
    vocab = w_vocab.shape[1]

    def vocab_logits(own, other, gain, weight, logits_out, stats_out):
        rows = []
        for part in range(2):
            mine = lax.axis_index("head") == part
            rows.append(jnp.where(mine, own[...], other[...]))
        rows = jnp.concatenate(rows, axis=1)
        scale = lax.rsqrt(jnp.mean(rows * rows, axis=1, keepdims=True) + EPS)
        rows = (rows * scale * gain[...]).astype(jnp.bfloat16)
        largest = None
        for start in range(0, vocab, 512):
            stop = min(start + 512, vocab)
            part = lax.dot_general(
                rows, weight[start:stop, :], (((1,), (1,)), ((), ())), preferred_element_type=jnp.float32
            )
            logits_out[:, start:stop] = part
            top = jnp.max(part, axis=1, keepdims=True)
            largest = top if largest is None else jnp.maximum(largest, top)
        total = jnp.sum(jnp.exp(logits_out[...] - largest), axis=1, keepdims=True)
        row = lax.broadcasted_iota(jnp.int32, (count, 128), 0)
        lane = lax.broadcasted_iota(jnp.int32, (count, 128), 1)
        stats = jnp.where(lane == row, largest, 0.0) + jnp.where(lane == row + 64, total, 0.0)
        stats_out[...] = jnp.broadcast_to(jnp.sum(stats, axis=0)[None, None], stats_out.shape)

    logits, stats = kernel_call(
        vocab_logits, [((count, vocab), jnp.float32), ((devices, 1, 128), jnp.float32)], 2 * count * w_vocab.size,
        "vocab_logits", half_rows, other_core(half_rows), final_gain[None, :],
        pltpu.with_memory_space_constraint(w_vocab.T, pltpu.VMEM),
    )
    corner_sent = []
    if corners:
        corner_outs = [(row_count * i, shape, jnp.bfloat16) for i in range(len(corners))]
        corner_pieces = summed([near[1]] + returned_corners, corner_outs, "corner_sum", gates=(stats,))
        corner_sent = [send(part, count, back(steps)) for part, steps in zip(corner_pieces, diagonal)]
    final = [residual, pieces[0]] + corner_sent + [
        send(part, count, back(steps)) for part, steps in zip(pieces[1:], outer)
    ]
    everyone = lax.all_to_all(stats, ("req", "head"), 0, 0, tiled=True)

    def finish(*refs):
        logits, everyone, hidden_out, log_out = *refs[:2], *refs[-2:]
        total = None
        for ref in refs[2:-2]:
            part = ref[...].astype(jnp.float32)
            total = part if total is None else total + part
        hidden_out[...] = total.astype(jnp.bfloat16)
        tiles = everyone[...]
        top = jnp.max(tiles, axis=0, keepdims=True)
        scaled = jnp.exp(jnp.minimum(tiles - top, 0.0))[:, :64] * tiles[:, 64:]
        shift = top[:, :64] + jnp.log(jnp.sum(scaled, axis=0, keepdims=True))
        row = lax.broadcasted_iota(jnp.int32, (count, 64), 0)
        lane = lax.broadcasted_iota(jnp.int32, (count, 64), 1)
        log_out[...] = logits[...] - jnp.sum(jnp.where(lane == row, shift, 0.0), axis=1, keepdims=True)

    outs = [(shape, jnp.bfloat16), ((count, vocab), jnp.float32)]
    return kernel_call(finish, outs, WEIGHT, "finish", logits, everyone[:, 0], *final, pinned=False)


def solution(mesh):
    in_specs = (
        P("req", None),
        P(),
        P(None, "head"),
        P(None, "head"),
        P(None, "head"),
        P(),
        P(),
        P("head", None),
        P("req", None, "head"),
        P("req", None, "head"),
        P(),
        P(),
        P("head"),
        P("head", "req"),
        P("head", "req"),
        P("req", "head"),
        P(),
        P(None, ("req", "head")),
    )
    out_specs = (P("req", "head"), P(None, ("req", "head")))
    return jax.shard_map(
        on_device, mesh=mesh, in_specs=in_specs, out_specs=out_specs, check_vma=False
    )
```

```python
import jax
import jax.numpy as jnp
import numpy as np
from jax import lax
from jax.experimental import pallas as pl
from jax.experimental.pallas import tpu as pltpu
from jax.sharding import PartitionSpec as P


HEAD_DIM = 128


EPS = 1e-06
ROPE_BASE = 1000000.0
NEG = -1e30
WEIGHT = 20000000000
VMEM_SPEC = pl.BlockSpec(memory_space=pltpu.VMEM)
LOG2E = 1.4426950408889634
SHIFT = 4.0
QUERY_PARTS, CACHE_PARTS, OUT_PARTS = 4, 1, 4


def sizes_of(count):
    if count == 16:
        return (4, 2, 2)
    side = round(count ** (1 / 3))
    if side**3 == count:
        return (side, side, side)
    return (count, 1, 1)


def moved(place, size, step):
    if size & (size - 1) == 0:
        return place ^ abs(step)
    return (place + step) % size


def send(rows, count, steps):
    sizes = sizes_of(count)
    pairs = []
    for i in range(count):
        target, left = 0, i
        places = []
        for size in reversed(sizes):
            places.append(left % size)
            left //= size
        for place, size, step in zip(reversed(places), sizes, steps):
            target = target * size + moved(place, size, step)
        pairs.append((i, target))
    return lax.ppermute(rows, "req", pairs)


def along(count, digit):
    steps = []
    for step in reversed(range(1, sizes_of(count)[digit])):
        one = [0, 0, 0]
        one[digit] = step
        steps.append(tuple(one))
    return steps


def across(count):
    return [(0, b[1], c[2]) for b in along(count, 1) for c in along(count, 2)]


def add_steps(one, two):
    return tuple(a + b for a, b in zip(one, two))


def slot_behind(slot, count, steps):
    result, stride = 0, 1
    for size, step in zip(reversed(sizes_of(count)), reversed(steps)):
        place = lax.rem(lax.div(slot, stride), size)
        if size & (size - 1) == 0:
            place = place ^ abs(step)
        else:
            place = lax.rem(place + size - step % size, size)
        result = result + place * stride
        stride *= size
    return result


def back(steps):
    return tuple(-step for step in steps)


def other_core(rows):
    return lax.ppermute(rows, "head", [(0, 1), (1, 0)])


def to_all(block, names):
    count = lax.axis_size(names)
    return lax.all_to_all(jnp.broadcast_to(block[None], (count,) + block.shape), names, 0, 0, tiled=True)


def kernel_call(body, outs, flops, name, *operands, gates=(), pinned=True):
    def run(*refs):
        body(*refs[: len(operands)], *refs[len(operands) + len(gates) :])

    result = pl.pallas_call(
        run,
        out_shape=tuple((pltpu.VMEM if pinned else jax.ShapeDtypeStruct)(shape, dtype) for shape, dtype in outs),
        in_specs=[VMEM_SPEC] * len(operands) + [pl.BlockSpec(memory_space=pl.ANY)] * len(gates),
        out_specs=(VMEM_SPEC,) * len(outs),
        compiler_params=pltpu.CompilerParams(vmem_limit_bytes=20 * 1024 * 1024),
        cost_estimate=pl.CostEstimate(flops=flops, bytes_accessed=1000000, transcendentals=0),
        name=name,
    )(*operands, *gates)
    return result


def attention_kernel(
    lengths_any,
    requests_any,
    hidden_any,
    attn_gain_any,
    query_gain_any,
    key_gain_any,
    frequency_any,
    w_query_any,
    w_key_any,
    w_value_any,
    cache_keys_any,
    cache_values_any,
    w_out_any,
    own_out,
    send_out,
    lengths,
    requests,
    hidden,
    attn_gain,
    query_gain,
    key_gain,
    frequency,
    w_query,
    w_key,
    w_value,
    cache_keys,
    cache_values,
    w_out,
    sems,
):
    copies = []

    def fetch(source, target, parts):
        rows = target.shape[0] // parts
        group = []
        for i in range(parts):
            copy = pltpu.make_async_copy(
                source.at[pl.ds(i * rows, rows)], target.at[pl.ds(i * rows, rows)], sems.at[len(copies)]
            )
            copy.start()
            copies.append(copy)
            group.append(copy)
        return group

    small_copies = fetch(hidden_any, hidden, 1) + fetch(requests_any, requests, 1)
    small_copies += fetch(lengths_any, lengths, 1) + fetch(frequency_any, frequency, 1)
    small_copies += fetch(attn_gain_any, attn_gain, 1) + fetch(query_gain_any, query_gain, 1)
    small_copies += fetch(key_gain_any, key_gain, 1)
    query_copies = fetch(w_query_any, w_query, QUERY_PARTS)
    key_copies = fetch(w_key_any, w_key, 2)
    value_copies = fetch(w_value_any, w_value, 2)
    cached_key_copies = fetch(cache_keys_any.at[0], cache_keys, CACHE_PARTS)
    cached_value_copies = fetch(cache_values_any.at[0], cache_values, CACHE_PARTS)
    out_copies = fetch(w_out_any, w_out, OUT_PARTS)

    row_count, width = hidden.shape
    query_heads = w_query.shape[1] // HEAD_DIM
    value_heads = w_key.shape[1] // HEAD_DIM
    group = query_heads // value_heads
    span = cache_keys.shape[0]
    for copy in small_copies:
        copy.wait()
    cache_len = lengths[requests[lax.axis_index("req")]]

    row = lax.broadcasted_iota(jnp.int32, (row_count, HEAD_DIM), 0)
    lane = lax.broadcasted_iota(jnp.int32, (row_count, HEAD_DIM), 1)
    angles = (row + cache_len).astype(jnp.float32) * frequency[...]
    cosine = jnp.cos(angles)
    sine = jnp.where(lane < HEAD_DIM // 2, -jnp.sin(angles), jnp.sin(angles))

    def turned(heads, gain):
        scale = lax.rsqrt(jnp.mean(heads * heads, axis=-1, keepdims=True) + EPS)
        heads = heads * scale * gain
        return (heads * cosine + pltpu.roll(heads, HEAD_DIM // 2, 1) * sine).astype(jnp.bfloat16)

    tokens = hidden[...].astype(jnp.float32)
    scale = lax.rsqrt(jnp.mean(tokens * tokens, axis=-1, keepdims=True) + EPS)
    normed = (tokens * scale * attn_gain[...]).astype(jnp.bfloat16)

    def project(weight, group_copies):
        rows = width // len(group_copies)
        total = None
        for i, copy in enumerate(group_copies):
            copy.wait()
            part = jnp.dot(
                normed[:, i * rows : (i + 1) * rows],
                weight[i * rows : (i + 1) * rows, :],
                preferred_element_type=jnp.float32,
            )
            total = part if total is None else total + part
        return total

    def head(field, h):
        return field[:, h * HEAD_DIM : (h + 1) * HEAD_DIM]

    projected = project(w_query, query_copies)
    queries = [turned(head(projected, h), query_gain[...]) for h in range(query_heads)]
    queries = [jnp.concatenate(queries[k * group : (k + 1) * group], axis=0) for k in range(value_heads)]
    projected = project(w_key, key_copies)
    keys_new = [turned(head(projected, k), key_gain[...]) for k in range(value_heads)]
    values_new = project(w_value, value_copies).astype(jnp.bfloat16)

    factor = HEAD_DIM**-0.5 * LOG2E
    contract = (((1,), (1,)), ((), ()))
    totals, blended = [], []
    query_row = lax.broadcasted_iota(jnp.int32, (group * row_count, row_count), 0) % row_count
    column = lax.broadcasted_iota(jnp.int32, (group * row_count, row_count), 1)
    causal = jnp.where(query_row >= column, -SHIFT, NEG)
    for k in range(value_heads):
        scores = lax.dot_general(queries[k], keys_new[k], contract, preferred_element_type=jnp.float32)
        weights = jnp.exp2(scores * factor + causal)
        totals.append(jnp.sum(weights, axis=-1, keepdims=True))
        blended.append(
            jnp.dot(weights.astype(jnp.bfloat16), head(values_new, k), preferred_element_type=jnp.float32)
        )
    rows = span // CACHE_PARTS
    place_in_cache = lax.broadcasted_iota(jnp.int32, (1, rows), 1)
    for i in range(CACHE_PARTS):
        cached_key_copies[i].wait()
        stored = jnp.where(place_in_cache + i * rows < cache_len, -SHIFT, NEG)
        part = []
        for k in range(value_heads):
            keys = cache_keys[i * rows : (i + 1) * rows, k * HEAD_DIM : (k + 1) * HEAD_DIM]
            scores = lax.dot_general(queries[k], keys, contract, preferred_element_type=jnp.float32)
            weights = jnp.exp2(scores * factor + stored)
            totals[k] = totals[k] + jnp.sum(weights, axis=-1, keepdims=True)
            part.append(weights.astype(jnp.bfloat16))
        cached_value_copies[i].wait()
        for k in range(value_heads):
            values = cache_values[i * rows : (i + 1) * rows, k * HEAD_DIM : (k + 1) * HEAD_DIM]
            blended[k] = blended[k] + jnp.dot(part[k], values, preferred_element_type=jnp.float32)
    attended = []
    for k in range(value_heads):
        result = (blended[k] / totals[k]).astype(jnp.bfloat16)
        attended += [result[g * row_count : (g + 1) * row_count] for g in range(group)]
    attended = jnp.concatenate(attended, axis=1)
    for copy in out_copies:
        copy.wait()
    projected = jnp.dot(attended, w_out[...], preferred_element_type=jnp.float32)
    own_out[...] = tokens + projected
    send_out[...] = projected.astype(jnp.bfloat16)


def attention_rows(
    hidden_in, attn_gain, w_query, w_key, w_value, query_gain, key_gain, w_out,
    cache_keys, cache_values, cache_lengths, slot_request,
):
    half = HEAD_DIM // 2
    frequency = ROPE_BASE ** (-2.0 * np.arange(half, dtype=np.float64) / HEAD_DIM)
    frequency = jnp.asarray(np.tile(frequency, 2)[None, :], jnp.float32)
    vmem = pl.BlockSpec(memory_space=pltpu.VMEM)
    anywhere = pl.BlockSpec(memory_space=pltpu.HBM)
    rows, width = hidden_in.shape
    return pl.pallas_call(
        attention_kernel,
        out_shape=(pltpu.VMEM((rows, width), jnp.float32), pltpu.VMEM((rows, width), jnp.bfloat16)),
        in_specs=[anywhere] * 13,
        out_specs=(vmem, vmem),
        scratch_shapes=[
            pltpu.SMEM(cache_lengths.shape, jnp.int32),
            pltpu.SMEM(slot_request.shape, jnp.int32),
            pltpu.VMEM(hidden_in.shape, jnp.bfloat16),
            pltpu.VMEM((1, width), jnp.float32),
            pltpu.VMEM((1, HEAD_DIM), jnp.float32),
            pltpu.VMEM((1, HEAD_DIM), jnp.float32),
            pltpu.VMEM((1, HEAD_DIM), jnp.float32),
            pltpu.VMEM(w_query.shape, jnp.bfloat16),
            pltpu.VMEM(w_key.shape, jnp.bfloat16),
            pltpu.VMEM(w_value.shape, jnp.bfloat16),
            pltpu.VMEM(cache_keys.shape[1:], jnp.bfloat16),
            pltpu.VMEM(cache_values.shape[1:], jnp.bfloat16),
            pltpu.VMEM(w_out.shape, jnp.bfloat16),
            pltpu.SemaphoreType.DMA((QUERY_PARTS + 11 + 2 * CACHE_PARTS + OUT_PARTS,)),
        ],
        compiler_params=pltpu.CompilerParams(vmem_limit_bytes=40 * 1024 * 1024),
        cost_estimate=pl.CostEstimate(flops=1400000000, bytes_accessed=17500000, transcendentals=1100000),
        name="attention_rows",
    )(*[
        pltpu.with_memory_space_constraint(operand, pltpu.HBM)
        for operand in (
            cache_lengths, slot_request, hidden_in, attn_gain[None, :], query_gain[None, :],
            key_gain[None, :], frequency, w_query, w_key, w_value, cache_keys, cache_values, w_out,
        )
    ])


def mix_rows(own, other, mlp_gain):
    rows, half = own.shape[0], mlp_gain.shape[1]

    def body(own, other, gain, mixed_out, residual_out):
        total = own[...] + other[...].astype(jnp.float32)
        scale = lax.rsqrt(jnp.mean(total * total, axis=1, keepdims=True) + EPS)
        for part in range(2):

            @pl.when(lax.axis_index("head") == part)
            def _():
                kept = total[:, part * half : (part + 1) * half]
                residual_out[...] = kept
                mixed_out[...] = (kept * scale * gain[...]).astype(jnp.bfloat16)

    outs = [((rows, half), jnp.bfloat16), ((rows, half), jnp.float32)]
    return kernel_call(body, outs, 1000000, "mix_rows", own, other, mlp_gain)


def stacked(blocks, name, gates=(), flops=1000000):
    rows, width = sum(block.shape[0] for block in blocks), blocks[0].shape[1]

    def body(*refs):
        start = 0
        for ref in refs[:-1]:
            refs[-1][start : start + ref.shape[0]] = ref[...]
            start += ref.shape[0]

    return kernel_call(body, [((rows, width), jnp.bfloat16)], flops, name, *blocks, gates=gates)[0]


def gate_up(blocks, w_gate, w_up, name, gates=()):
    rows, units = sum(block.shape[0] for block in blocks), w_gate.shape[1]

    def body(*refs):
        start = 0
        w_gate, w_up, own_out, send_out = refs[-4:]
        for ref in refs[:-4]:
            for i, weight in enumerate((w_gate, w_up)):
                part = jnp.dot(ref[...], weight[...], preferred_element_type=jnp.float32)
                own_out[i, start : start + ref.shape[0]] = part
                send_out[i, start : start + ref.shape[0]] = part.astype(jnp.bfloat16)
            start += ref.shape[0]

    outs = [((2, rows, units), jnp.float32), ((2, rows, units), jnp.bfloat16)]
    flops = 4 * rows * w_gate.size
    return kernel_call(body, outs, flops, name, *blocks, w_gate, w_up, gates=gates)


def down_parts(own, other, w_down, outs, name, gates=()):
    rows = own.shape[1]

    def body(own, other, w_down, *out_refs):
        gate = own[0] + other[0].astype(jnp.float32)
        up = own[1] + other[1].astype(jnp.float32)
        active = (gate / (1.0 + jnp.exp(-gate)) * up).astype(jnp.bfloat16)
        start = 0
        for ref in out_refs:
            stop = start + ref.shape[0]
            part = jnp.dot(active[start:stop], w_down[...], preferred_element_type=jnp.float32)
            ref[...] = part.astype(ref.dtype)
            start = stop

    return kernel_call(body, outs, 2 * rows * w_down.size, name, own, other, w_down, gates=gates)


def summed(terms, outs, name, gates=(), flops=1000000, pinned=True):
    def body(*refs):
        total = None
        for ref in refs[: len(terms)]:
            part = ref[...].astype(jnp.float32)
            total = part if total is None else total + part
        for ref, (start, shape, dtype) in zip(refs[len(terms) :], outs):
            ref[...] = total[start : start + shape[0]].astype(dtype)

    plain = [(shape, dtype) for _, shape, dtype in outs]
    return kernel_call(body, plain, flops, name, *terms, gates=gates, pinned=pinned)


def on_device(
    hidden_in,
    attn_gain,
    w_query,
    w_key,
    w_value,
    query_gain,
    key_gain,
    w_out,
    cache_keys,
    cache_values,
    cache_lengths,
    slot_request,
    mlp_gain,
    w_gate,
    w_up,
    w_down,
    final_gain,
    w_vocab,
):
    row_count = hidden_in.shape[0]
    half_width = mlp_gain.shape[0]
    count = lax.axis_size("req")
    own, sent = attention_rows(
        hidden_in, attn_gain, w_query, w_key, w_value, query_gain, key_gain, w_out,
        cache_keys, cache_values, cache_lengths, slot_request,
    )
    mixed, residual = mix_rows(own, other_core(sent), mlp_gain[None, :])
    shape = mixed.shape
    outer, middle, inner, diagonal = along(count, 0), along(count, 1), along(count, 2), across(count)

    columns = [send(mixed, count, steps) for steps in outer]
    corners = [send(mixed, count, steps) for steps in diagonal]
    column = stacked([mixed] + columns, "column", gates=corners)
    corner = stacked(corners, "corner") if len(corners) > 1 else corners[0] if corners else None
    far = [send(column, count, steps) for steps in inner + middle]
    far_corners = [send(corner, count, steps) for steps in outer] if corners else []

    near_own, near_sent = gate_up([column] + ([corner] if corners else []), w_gate, w_up, "near_gate_up")
    near_rows = near_own.shape[1]
    near_outs = [(column.shape, jnp.float32)] + ([(corner.shape, jnp.float32)] if corners else [])
    near = down_parts(near_own, other_core(near_sent), w_down, near_outs, "near_down")

    far_corner = []
    if corners:
        far_corner = [stacked(far_corners, "far_corner", gates=(near_own,), flops=WEIGHT)]
        far = lax.optimization_barrier((far, far_corner))[0]

    at_home = (0, 0, 0)
    places = [at_home] + outer + diagonal
    for steps in inner + middle:
        places += [add_steps(steps, line) for line in [at_home] + outer]
    for steps in outer if corners else []:
        places += [add_steps(steps, turn) for turn in diagonal]
    last_shape = (count, half_width)
    blocks = [column] + ([corner] if corners else []) + far + far_corner

    def request_of(steps, requests):
        slots = lax.broadcasted_iota(jnp.int32, (1, count), 1)
        slot = slot_behind(lax.axis_index("req"), count, steps)
        return jnp.sum(jnp.where(slots == slot, requests[...], 0), axis=1, keepdims=True)

    def last_gate_up(*refs):
        requests, w_gate, w_up, own_out, send_out = refs[-5:]
        order = lax.broadcasted_iota(jnp.int32, (count, 1), 0)
        rows, place = jnp.zeros(last_shape, jnp.float32), 0
        for ref in refs[:-5]:
            for stop in range(row_count, ref.shape[0] + 1, row_count):
                last = ref[stop - 16 : stop].astype(jnp.float32)[15:]
                rows = rows + jnp.where(order == request_of(places[place], requests), last, 0.0)
                place += 1
        rows = rows.astype(jnp.bfloat16)
        for i, weight in enumerate((w_gate, w_up)):
            part = jnp.dot(rows, weight[...], preferred_element_type=jnp.float32)
            own_out[i] = part
            send_out[i] = part.astype(jnp.bfloat16)

    units = w_gate.shape[1]
    last_own, last_sent = kernel_call(
        last_gate_up, [((2, count, units), jnp.float32), ((2, count, units), jnp.bfloat16)], 100000000,
        "last_gate_up", *blocks, slot_request[None, :], w_gate, w_up,
    )
    def last_down(own, other, w_down, residual, requests, kept_out, sent_out):
        gate = own[0] + other[0].astype(jnp.float32)
        up = own[1] + other[1].astype(jnp.float32)
        active = (gate / (1.0 + jnp.exp(-gate)) * up).astype(jnp.bfloat16)
        order = lax.broadcasted_iota(jnp.int32, (count, 1), 0)
        total = jnp.dot(active, w_down[...], preferred_element_type=jnp.float32)
        total = total + jnp.where(order == request_of(at_home, requests), residual[row_count - 1 :, :], 0.0)
        kept_out[...] = total
        sent_out[...] = total.astype(jnp.bfloat16)

    last_outs = [(last_shape, jnp.float32), (last_shape, jnp.bfloat16)]
    last_kept, last_sent = kernel_call(
        last_down, last_outs, 100000000, "last_down",
        last_own, other_core(last_sent), w_down, residual, slot_request[None, :],
    )
    far_own, far_sent = gate_up(far + far_corner, w_gate, w_up, "far_gate_up", gates=(near[0], last_sent))
    last_lines = [send(last_sent, count, steps) for steps in outer]
    last_outs = [(0, last_shape, jnp.float32), (0, last_shape, jnp.bfloat16)]
    far_outs = [(column.shape, jnp.bfloat16) for _ in far] + [(corner.shape, jnp.bfloat16) for _ in far_corners]
    parts = down_parts(far_own, other_core(far_sent), w_down, far_outs, "far_down")
    last_outs = [(0, last_shape, jnp.float32), (0, last_shape, jnp.bfloat16)]

    def join_lines(*refs):
        lines, sources = refs[1 : 1 + len(outer)], refs[1 + len(outer) : 1 + len(outer) + len(far)]
        kept_out, sent_out, *packed_outs = refs[1 + len(outer) + len(far) :]
        total = refs[0][...]
        for ref in lines:
            total = total + ref[...].astype(jnp.float32)
        kept_out[...] = total
        sent_out[...] = total.astype(jnp.bfloat16)
        for source, ref in zip(sources, packed_outs):
            ref[: source.shape[0]] = source[...]
            ref[source.shape[0] :] = total.astype(jnp.bfloat16)

    column_rows = column.shape[0]
    packed_out = ((column_rows + count, half_width), jnp.bfloat16)
    last_kept, last_sent, *packed = kernel_call(
        join_lines, [(last_shape, jnp.float32), (last_shape, jnp.bfloat16)] + [packed_out] * len(far), 1000000,
        "join_lines", last_kept, *last_lines, *parts[: len(far)],
    )

    returned = [send(part, count, back(steps)) for part, steps in zip(packed, inner + middle)]
    last_corners = [send(last_sent, count, steps) for steps in diagonal]
    far_parts = parts[len(far) :]
    returned_corners = [send(part, count, back(steps)) for part, steps in zip(far_parts, outer)]

    def join_columns(*refs):
        own, last, sums = refs[0], refs[1], refs[2 : 2 + len(far)]
        turns, out_refs = refs[2 + len(far) : 2 + len(far) + len(diagonal)], refs[2 + len(far) + len(diagonal) :]
        for i, ref in enumerate(out_refs[:-1]):
            rows = slice(i * row_count, (i + 1) * row_count)
            total = own[rows]
            for part in sums:
                total = total + part[rows].astype(jnp.float32)
            ref[...] = total.astype(ref.dtype)
        total = last[...]
        for part in sums:
            total = total + part[column_rows:].astype(jnp.float32)
        for part in turns:
            total = total + part[...].astype(jnp.float32)
        out_refs[-1][...] = total

    column_outs = [(shape, jnp.float32)] + [(shape, jnp.bfloat16)] * len(outer) + [(last_shape, jnp.float32)]
    *pieces, half_rows = kernel_call(
        join_columns, column_outs, 1000000, "join_columns", near[0], last_kept, *returned, *last_corners,
    )
    devices = count * lax.axis_size("head")
    vocab = w_vocab.shape[1]

    def vocab_logits(own, other, gain, weight, logits_out, stats_out):
        rows = []
        for part in range(2):
            mine = lax.axis_index("head") == part
            rows.append(jnp.where(mine, own[...], other[...]))
        rows = jnp.concatenate(rows, axis=1)
        scale = lax.rsqrt(jnp.mean(rows * rows, axis=1, keepdims=True) + EPS)
        rows = (rows * scale * gain[...]).astype(jnp.bfloat16)
        largest = None
        for start in range(0, vocab, 512):
            stop = min(start + 512, vocab)
            part = lax.dot_general(
                rows, weight[start:stop, :], (((1,), (1,)), ((), ())), preferred_element_type=jnp.float32
            )
            logits_out[:, start:stop] = part
            top = jnp.max(part, axis=1, keepdims=True)
            largest = top if largest is None else jnp.maximum(largest, top)
        total = jnp.sum(jnp.exp(logits_out[...] - largest), axis=1, keepdims=True)
        row = lax.broadcasted_iota(jnp.int32, (count, 128), 0)
        lane = lax.broadcasted_iota(jnp.int32, (count, 128), 1)
        stats = jnp.where(lane == row, largest, 0.0) + jnp.where(lane == row + 64, total, 0.0)
        stats_out[...] = jnp.broadcast_to(jnp.sum(stats, axis=0)[None, None], stats_out.shape)

    logits, stats = kernel_call(
        vocab_logits, [((count, vocab), jnp.float32), ((devices, 1, 128), jnp.float32)], 2 * count * w_vocab.size,
        "vocab_logits", half_rows, other_core(half_rows), final_gain[None, :],
        pltpu.with_memory_space_constraint(w_vocab.T, pltpu.VMEM),
    )
    corner_sent = []
    if corners:
        corner_outs = [(row_count * i, shape, jnp.bfloat16) for i in range(len(corners))]
        corner_pieces = summed([near[1]] + returned_corners, corner_outs, "corner_sum", gates=(stats,))
        corner_sent = [send(part, count, back(steps)) for part, steps in zip(corner_pieces, diagonal)]
    final = [residual, pieces[0]] + corner_sent + [
        send(part, count, back(steps)) for part, steps in zip(pieces[1:], outer)
    ]
    everyone = lax.all_to_all(stats, ("req", "head"), 0, 0, tiled=True)

    def finish(*refs):
        logits, everyone, hidden_out, log_out = *refs[:2], *refs[-2:]
        total = None
        for ref in refs[2:-2]:
            part = ref[...].astype(jnp.float32)
            total = part if total is None else total + part
        hidden_out[...] = total.astype(jnp.bfloat16)
        tiles = everyone[...]
        top = jnp.max(tiles, axis=0, keepdims=True)
        scaled = jnp.exp(jnp.minimum(tiles - top, 0.0))[:, :64] * tiles[:, 64:]
        spread = jnp.log(jnp.sum(scaled, axis=0, keepdims=True))
        row = lax.broadcasted_iota(jnp.int32, (count, 64), 0)
        lane = lax.broadcasted_iota(jnp.int32, (count, 64), 1)
        largest = jnp.sum(jnp.where(lane == row, top[:, :64], 0.0), axis=1, keepdims=True)
        spread = jnp.sum(jnp.where(lane == row, spread, 0.0), axis=1, keepdims=True)
        log_out[...] = (logits[...] - largest) - spread

    outs = [(shape, jnp.bfloat16), ((count, vocab), jnp.float32)]
    return kernel_call(finish, outs, 1000000, "finish", logits, everyone[:, 0], *final, pinned=False)


def solution(mesh):
    in_specs = (
        P("req", None),
        P(),
        P(None, "head"),
        P(None, "head"),
        P(None, "head"),
        P(),
        P(),
        P("head", None),
        P("req", None, "head"),
        P("req", None, "head"),
        P(),
        P(),
        P("head"),
        P("head", "req"),
        P("head", "req"),
        P("req", "head"),
        P(),
        P(None, ("req", "head")),
    )
    out_specs = (P("req", "head"), P(None, ("req", "head")))
    return jax.shard_map(
        on_device, mesh=mesh, in_specs=in_specs, out_specs=out_specs, check_vma=False
    )
```

```python
import jax
import jax.numpy as jnp
import numpy as np
from jax import lax
from jax.experimental import pallas as pl
from jax.experimental.pallas import tpu as pltpu
from jax.sharding import PartitionSpec as P


HEAD_DIM = 128


EPS = 1e-06
ROPE_BASE = 1000000.0
NEG = -1e30
WEIGHT = 20000000000
VMEM_SPEC = pl.BlockSpec(memory_space=pltpu.VMEM)
LOG2E = 1.4426950408889634
SHIFT = 4.0
QUERY_PARTS, CACHE_PARTS, OUT_PARTS = 4, 1, 4


def sizes_of(count):
    if count == 16:
        return (4, 2, 2)
    side = round(count ** (1 / 3))
    if side**3 == count:
        return (side, side, side)
    return (count, 1, 1)


def moved(place, size, step):
    if size & (size - 1) == 0:
        return place ^ abs(step)
    return (place + step) % size


def send(rows, count, steps):
    sizes = sizes_of(count)
    pairs = []
    for i in range(count):
        target, left = 0, i
        places = []
        for size in reversed(sizes):
            places.append(left % size)
            left //= size
        for place, size, step in zip(reversed(places), sizes, steps):
            target = target * size + moved(place, size, step)
        pairs.append((i, target))
    return lax.ppermute(rows, "req", pairs)


def along(count, digit):
    steps = []
    for step in reversed(range(1, sizes_of(count)[digit])):
        one = [0, 0, 0]
        one[digit] = step
        steps.append(tuple(one))
    return steps


def across(count):
    return [(0, b[1], c[2]) for b in along(count, 1) for c in along(count, 2)]


def add_steps(one, two):
    return tuple(a + b for a, b in zip(one, two))


def slot_behind(slot, count, steps):
    result, stride = 0, 1
    for size, step in zip(reversed(sizes_of(count)), reversed(steps)):
        place = lax.rem(lax.div(slot, stride), size)
        if size & (size - 1) == 0:
            place = place ^ abs(step)
        else:
            place = lax.rem(place + size - step % size, size)
        result = result + place * stride
        stride *= size
    return result


def back(steps):
    return tuple(-step for step in steps)


def other_core(rows):
    return lax.ppermute(rows, "head", [(0, 1), (1, 0)])


def to_all(block, names):
    count = lax.axis_size(names)
    return lax.all_to_all(jnp.broadcast_to(block[None], (count,) + block.shape), names, 0, 0, tiled=True)


def kernel_call(body, outs, flops, name, *operands, gates=(), pinned=True):
    def run(*refs):
        body(*refs[: len(operands)], *refs[len(operands) + len(gates) :])

    result = pl.pallas_call(
        run,
        out_shape=tuple((pltpu.VMEM if pinned else jax.ShapeDtypeStruct)(shape, dtype) for shape, dtype in outs),
        in_specs=[VMEM_SPEC] * len(operands) + [pl.BlockSpec(memory_space=pl.ANY)] * len(gates),
        out_specs=(VMEM_SPEC,) * len(outs),
        compiler_params=pltpu.CompilerParams(vmem_limit_bytes=20 * 1024 * 1024),
        cost_estimate=pl.CostEstimate(flops=flops, bytes_accessed=1000000, transcendentals=0),
        name=name,
    )(*operands, *gates)
    return result


def attention_kernel(
    lengths_any,
    requests_any,
    hidden_any,
    attn_gain_any,
    query_gain_any,
    key_gain_any,
    frequency_any,
    w_query_any,
    w_key_any,
    w_value_any,
    cache_keys_any,
    cache_values_any,
    w_out_any,
    own_out,
    send_out,
    lengths,
    requests,
    hidden,
    attn_gain,
    query_gain,
    key_gain,
    frequency,
    w_query,
    w_key,
    w_value,
    cache_keys,
    cache_values,
    w_out,
    sems,
):
    copies = []

    def fetch(source, target, parts):
        rows = target.shape[0] // parts
        group = []
        for i in range(parts):
            copy = pltpu.make_async_copy(
                source.at[pl.ds(i * rows, rows)], target.at[pl.ds(i * rows, rows)], sems.at[len(copies)]
            )
            copy.start()
            copies.append(copy)
            group.append(copy)
        return group

    small_copies = fetch(hidden_any, hidden, 1) + fetch(requests_any, requests, 1)
    small_copies += fetch(lengths_any, lengths, 1) + fetch(frequency_any, frequency, 1)
    small_copies += fetch(attn_gain_any, attn_gain, 1) + fetch(query_gain_any, query_gain, 1)
    small_copies += fetch(key_gain_any, key_gain, 1)
    query_copies = fetch(w_query_any, w_query, QUERY_PARTS)
    key_copies = fetch(w_key_any, w_key, 2)
    value_copies = fetch(w_value_any, w_value, 2)
    cached_key_copies = fetch(cache_keys_any.at[0], cache_keys, CACHE_PARTS)
    cached_value_copies = fetch(cache_values_any.at[0], cache_values, CACHE_PARTS)
    out_copies = fetch(w_out_any, w_out, OUT_PARTS)

    row_count, width = hidden.shape
    query_heads = w_query.shape[1] // HEAD_DIM
    value_heads = w_key.shape[1] // HEAD_DIM
    group = query_heads // value_heads
    span = cache_keys.shape[0]
    for copy in small_copies:
        copy.wait()
    cache_len = lengths[requests[lax.axis_index("req")]]

    row = lax.broadcasted_iota(jnp.int32, (row_count, HEAD_DIM), 0)
    lane = lax.broadcasted_iota(jnp.int32, (row_count, HEAD_DIM), 1)
    angles = (row + cache_len).astype(jnp.float32) * frequency[...]
    cosine = jnp.cos(angles)
    sine = jnp.sin(angles)
    sine = jnp.where(lane < HEAD_DIM // 2, -sine, sine)

    def turned(heads, gain):
        scale = lax.rsqrt(jnp.mean(heads * heads, axis=-1, keepdims=True) + EPS)
        heads = heads * scale * gain
        return (heads * cosine + pltpu.roll(heads, HEAD_DIM // 2, 1) * sine).astype(jnp.bfloat16)

    tokens = hidden[...].astype(jnp.float32)
    scale = lax.rsqrt(jnp.mean(tokens * tokens, axis=-1, keepdims=True) + EPS)
    normed = (tokens * scale * attn_gain[...]).astype(jnp.bfloat16)

    def project(weight, group_copies):
        rows = width // len(group_copies)
        total = None
        for i, copy in enumerate(group_copies):
            copy.wait()
            part = jnp.dot(
                normed[:, i * rows : (i + 1) * rows],
                weight[i * rows : (i + 1) * rows, :],
                preferred_element_type=jnp.float32,
            )
            total = part if total is None else total + part
        return total

    def head(field, h):
        return field[:, h * HEAD_DIM : (h + 1) * HEAD_DIM]

    projected = project(w_query, query_copies)
    queries = [turned(head(projected, h), query_gain[...]) for h in range(query_heads)]
    queries = [jnp.concatenate(queries[k * group : (k + 1) * group], axis=0) for k in range(value_heads)]
    projected = project(w_key, key_copies)
    keys_new = [turned(head(projected, k), key_gain[...]) for k in range(value_heads)]
    values_new = project(w_value, value_copies).astype(jnp.bfloat16)

    factor = HEAD_DIM**-0.5 * LOG2E
    contract = (((1,), (1,)), ((), ()))
    totals, blended = [], []
    query_row = lax.broadcasted_iota(jnp.int32, (group * row_count, row_count), 0) % row_count
    column = lax.broadcasted_iota(jnp.int32, (group * row_count, row_count), 1)
    causal = jnp.where(query_row >= column, -SHIFT, NEG)
    for k in range(value_heads):
        scores = lax.dot_general(queries[k], keys_new[k], contract, preferred_element_type=jnp.float32)
        weights = jnp.exp2(scores * factor + causal)
        totals.append(jnp.sum(weights, axis=-1, keepdims=True))
        blended.append(
            jnp.dot(weights.astype(jnp.bfloat16), head(values_new, k), preferred_element_type=jnp.float32)
        )
    rows = span // CACHE_PARTS
    place_in_cache = lax.broadcasted_iota(jnp.int32, (1, rows), 1)
    for i in range(CACHE_PARTS):
        cached_key_copies[i].wait()
        stored = jnp.where(place_in_cache + i * rows < cache_len, -SHIFT, NEG)
        part = []
        for k in range(value_heads):
            keys = cache_keys[i * rows : (i + 1) * rows, k * HEAD_DIM : (k + 1) * HEAD_DIM]
            scores = lax.dot_general(queries[k], keys, contract, preferred_element_type=jnp.float32)
            weights = jnp.exp2(scores * factor + stored)
            totals[k] = totals[k] + jnp.sum(weights, axis=-1, keepdims=True)
            part.append(weights.astype(jnp.bfloat16))
        cached_value_copies[i].wait()
        for k in range(value_heads):
            values = cache_values[i * rows : (i + 1) * rows, k * HEAD_DIM : (k + 1) * HEAD_DIM]
            blended[k] = blended[k] + jnp.dot(part[k], values, preferred_element_type=jnp.float32)
    attended = []
    for k in range(value_heads):
        result = (blended[k] / totals[k]).astype(jnp.bfloat16)
        attended += [result[g * row_count : (g + 1) * row_count] for g in range(group)]
    attended = jnp.concatenate(attended, axis=1)
    for copy in out_copies:
        copy.wait()
    projected = jnp.dot(attended, w_out[...], preferred_element_type=jnp.float32)
    own_out[...] = tokens + projected
    send_out[...] = projected.astype(jnp.bfloat16)


def attention_rows(
    hidden_in, attn_gain, w_query, w_key, w_value, query_gain, key_gain, w_out,
    cache_keys, cache_values, cache_lengths, slot_request,
):
    half = HEAD_DIM // 2
    frequency = ROPE_BASE ** (-2.0 * np.arange(half, dtype=np.float64) / HEAD_DIM)
    frequency = jnp.asarray(np.tile(frequency, 2)[None, :], jnp.float32)
    vmem = pl.BlockSpec(memory_space=pltpu.VMEM)
    anywhere = pl.BlockSpec(memory_space=pltpu.HBM)
    rows, width = hidden_in.shape
    return pl.pallas_call(
        attention_kernel,
        out_shape=(pltpu.VMEM((rows, width), jnp.float32), pltpu.VMEM((rows, width), jnp.bfloat16)),
        in_specs=[anywhere] * 13,
        out_specs=(vmem, vmem),
        scratch_shapes=[
            pltpu.SMEM(cache_lengths.shape, jnp.int32),
            pltpu.SMEM(slot_request.shape, jnp.int32),
            pltpu.VMEM(hidden_in.shape, jnp.bfloat16),
            pltpu.VMEM((1, width), jnp.float32),
            pltpu.VMEM((1, HEAD_DIM), jnp.float32),
            pltpu.VMEM((1, HEAD_DIM), jnp.float32),
            pltpu.VMEM((1, HEAD_DIM), jnp.float32),
            pltpu.VMEM(w_query.shape, jnp.bfloat16),
            pltpu.VMEM(w_key.shape, jnp.bfloat16),
            pltpu.VMEM(w_value.shape, jnp.bfloat16),
            pltpu.VMEM(cache_keys.shape[1:], jnp.bfloat16),
            pltpu.VMEM(cache_values.shape[1:], jnp.bfloat16),
            pltpu.VMEM(w_out.shape, jnp.bfloat16),
            pltpu.SemaphoreType.DMA((QUERY_PARTS + 11 + 2 * CACHE_PARTS + OUT_PARTS,)),
        ],
        compiler_params=pltpu.CompilerParams(vmem_limit_bytes=40 * 1024 * 1024),
        cost_estimate=pl.CostEstimate(flops=1400000000, bytes_accessed=17500000, transcendentals=1100000),
        name="attention_rows",
    )(*[
        pltpu.with_memory_space_constraint(operand, pltpu.HBM)
        for operand in (
            cache_lengths, slot_request, hidden_in, attn_gain[None, :], query_gain[None, :],
            key_gain[None, :], frequency, w_query, w_key, w_value, cache_keys, cache_values, w_out,
        )
    ])


def mix_rows(own, other, mlp_gain):
    rows, half = own.shape[0], mlp_gain.shape[1]

    def body(own, other, gain, mixed_out, residual_out):
        total = own[...] + other[...].astype(jnp.float32)
        scale = lax.rsqrt(jnp.mean(total * total, axis=1, keepdims=True) + EPS)
        for part in range(2):

            @pl.when(lax.axis_index("head") == part)
            def _():
                kept = total[:, part * half : (part + 1) * half]
                residual_out[...] = kept
                mixed_out[...] = (kept * scale * gain[...]).astype(jnp.bfloat16)

    outs = [((rows, half), jnp.bfloat16), ((rows, half), jnp.float32)]
    return kernel_call(body, outs, 1000000, "mix_rows", own, other, mlp_gain)


def stacked(blocks, name, gates=(), flops=1000000):
    rows, width = sum(block.shape[0] for block in blocks), blocks[0].shape[1]

    def body(*refs):
        start = 0
        for ref in refs[:-1]:
            refs[-1][start : start + ref.shape[0]] = ref[...]
            start += ref.shape[0]

    return kernel_call(body, [((rows, width), jnp.bfloat16)], flops, name, *blocks, gates=gates)[0]


def gate_up(blocks, w_gate, w_up, name, gates=()):
    rows, units = sum(block.shape[0] for block in blocks), w_gate.shape[1]

    def body(*refs):
        start = 0
        w_gate, w_up, own_out, send_out = refs[-4:]
        for ref in refs[:-4]:
            for i, weight in enumerate((w_gate, w_up)):
                part = jnp.dot(ref[...], weight[...], preferred_element_type=jnp.float32)
                own_out[i, start : start + ref.shape[0]] = part
                send_out[i, start : start + ref.shape[0]] = part.astype(jnp.bfloat16)
            start += ref.shape[0]

    outs = [((2, rows, units), jnp.float32), ((2, rows, units), jnp.bfloat16)]
    flops = 4 * rows * w_gate.size
    return kernel_call(body, outs, flops, name, *blocks, w_gate, w_up, gates=gates)


def down_parts(own, other, w_down, outs, name, gates=()):
    rows = own.shape[1]

    def body(own, other, w_down, *out_refs):
        gate = own[0] + other[0].astype(jnp.float32)
        up = own[1] + other[1].astype(jnp.float32)
        active = (gate / (1.0 + jnp.exp(-gate)) * up).astype(jnp.bfloat16)
        start = 0
        for ref in out_refs:
            stop = start + ref.shape[0]
            part = jnp.dot(active[start:stop], w_down[...], preferred_element_type=jnp.float32)
            ref[...] = part.astype(ref.dtype)
            start = stop

    return kernel_call(body, outs, 2 * rows * w_down.size, name, own, other, w_down, gates=gates)


def summed(terms, outs, name, gates=(), flops=1000000, pinned=True):
    def body(*refs):
        total = None
        for ref in refs[: len(terms)]:
            part = ref[...].astype(jnp.float32)
            total = part if total is None else total + part
        for ref, (start, shape, dtype) in zip(refs[len(terms) :], outs):
            ref[...] = total[start : start + shape[0]].astype(dtype)

    plain = [(shape, dtype) for _, shape, dtype in outs]
    return kernel_call(body, plain, flops, name, *terms, gates=gates, pinned=pinned)


def on_device(
    hidden_in,
    attn_gain,
    w_query,
    w_key,
    w_value,
    query_gain,
    key_gain,
    w_out,
    cache_keys,
    cache_values,
    cache_lengths,
    slot_request,
    mlp_gain,
    w_gate,
    w_up,
    w_down,
    final_gain,
    w_vocab,
):
    row_count = hidden_in.shape[0]
    half_width = mlp_gain.shape[0]
    count = lax.axis_size("req")
    own, sent = attention_rows(
        hidden_in, attn_gain, w_query, w_key, w_value, query_gain, key_gain, w_out,
        cache_keys, cache_values, cache_lengths, slot_request,
    )
    mixed, residual = mix_rows(own, other_core(sent), mlp_gain[None, :])
    shape = mixed.shape
    outer, middle, inner, diagonal = along(count, 0), along(count, 1), along(count, 2), across(count)

    columns = [send(mixed, count, steps) for steps in outer]
    corners = [send(mixed, count, steps) for steps in diagonal]
    column = stacked([mixed] + columns, "column", gates=corners, flops=WEIGHT)
    corner = stacked(corners, "corner") if len(corners) > 1 else corners[0] if corners else None
    far = [send(column, count, steps) for steps in inner + middle]
    far_corners = [send(corner, count, steps) for steps in outer] if corners else []

    near_own, near_sent = gate_up([column] + ([corner] if corners else []), w_gate, w_up, "near_gate_up")
    near_rows = near_own.shape[1]
    near_outs = [(column.shape, jnp.float32)] + ([(corner.shape, jnp.float32)] if corners else [])
    near = down_parts(near_own, other_core(near_sent), w_down, near_outs, "near_down")

    far_corner = []
    if corners:
        far_corner = [stacked(far_corners, "far_corner", gates=(near_own,), flops=WEIGHT)]
        far = lax.optimization_barrier((far, far_corner))[0]

    at_home = (0, 0, 0)
    places = [at_home] + outer + diagonal
    for steps in inner + middle:
        places += [add_steps(steps, line) for line in [at_home] + outer]
    for steps in outer if corners else []:
        places += [add_steps(steps, turn) for turn in diagonal]
    last_shape = (count, half_width)
    blocks = [column] + ([corner] if corners else []) + far + far_corner

    def request_of(steps, requests):
        slots = lax.broadcasted_iota(jnp.int32, (1, count), 1)
        slot = slot_behind(lax.axis_index("req"), count, steps)
        return jnp.sum(jnp.where(slots == slot, requests[...], 0), axis=1, keepdims=True)

    def last_gate_up(*refs):
        requests, w_gate, w_up, own_out, send_out = refs[-5:]
        order = lax.broadcasted_iota(jnp.int32, (count, 1), 0)
        rows, place = jnp.zeros(last_shape, jnp.float32), 0
        for ref in refs[:-5]:
            for stop in range(row_count, ref.shape[0] + 1, row_count):
                last = ref[stop - 16 : stop].astype(jnp.float32)[15:]
                rows = rows + jnp.where(order == request_of(places[place], requests), last, 0.0)
                place += 1
        rows = rows.astype(jnp.bfloat16)
        for i, weight in enumerate((w_gate, w_up)):
            part = jnp.dot(rows, weight[...], preferred_element_type=jnp.float32)
            own_out[i] = part
            send_out[i] = part.astype(jnp.bfloat16)

    units = w_gate.shape[1]
    last_own, last_sent = kernel_call(
        last_gate_up, [((2, count, units), jnp.float32), ((2, count, units), jnp.bfloat16)], 100000000,
        "last_gate_up", *blocks, slot_request[None, :], w_gate, w_up,
    )
    def last_down(own, other, w_down, residual, requests, kept_out, sent_out):
        gate = own[0] + other[0].astype(jnp.float32)
        up = own[1] + other[1].astype(jnp.float32)
        active = (gate / (1.0 + jnp.exp(-gate)) * up).astype(jnp.bfloat16)
        order = lax.broadcasted_iota(jnp.int32, (count, 1), 0)
        total = jnp.dot(active, w_down[...], preferred_element_type=jnp.float32)
        total = total + jnp.where(order == request_of(at_home, requests), residual[row_count - 1 :, :], 0.0)
        kept_out[...] = total
        sent_out[...] = total.astype(jnp.bfloat16)

    last_outs = [(last_shape, jnp.float32), (last_shape, jnp.bfloat16)]
    last_kept, last_sent = kernel_call(
        last_down, last_outs, 100000000, "last_down",
        last_own, other_core(last_sent), w_down, residual, slot_request[None, :],
    )
    far_own, far_sent = gate_up(far + far_corner, w_gate, w_up, "far_gate_up", gates=(near[0], last_sent))
    last_lines = [send(last_sent, count, steps) for steps in outer]
    last_outs = [(0, last_shape, jnp.float32), (0, last_shape, jnp.bfloat16)]
    far_outs = [(column.shape, jnp.bfloat16) for _ in far] + [(corner.shape, jnp.bfloat16) for _ in far_corners]
    parts = down_parts(far_own, other_core(far_sent), w_down, far_outs, "far_down")
    last_outs = [(0, last_shape, jnp.float32), (0, last_shape, jnp.bfloat16)]

    def join_lines(*refs):
        lines, sources = refs[1 : 1 + len(outer)], refs[1 + len(outer) : 1 + len(outer) + len(far)]
        kept_out, sent_out, *packed_outs = refs[1 + len(outer) + len(far) :]
        total = refs[0][...]
        for ref in lines:
            total = total + ref[...].astype(jnp.float32)
        kept_out[...] = total
        sent_out[...] = total.astype(jnp.bfloat16)
        for source, ref in zip(sources, packed_outs):
            ref[: source.shape[0]] = source[...]
            ref[source.shape[0] :] = total.astype(jnp.bfloat16)

    column_rows = column.shape[0]
    packed_out = ((column_rows + count, half_width), jnp.bfloat16)
    last_kept, last_sent, *packed = kernel_call(
        join_lines, [(last_shape, jnp.float32), (last_shape, jnp.bfloat16)] + [packed_out] * len(far), 1000000,
        "join_lines", last_kept, *last_lines, *parts[: len(far)],
    )

    returned = [send(part, count, back(steps)) for part, steps in zip(packed, inner + middle)]
    last_corners = [send(last_sent, count, steps) for steps in diagonal]
    far_parts = parts[len(far) :]
    returned_corners = [send(part, count, back(steps)) for part, steps in zip(far_parts, outer)]

    def join_columns(*refs):
        own, last, sums = refs[0], refs[1], refs[2 : 2 + len(far)]
        turns, out_refs = refs[2 + len(far) : 2 + len(far) + len(diagonal)], refs[2 + len(far) + len(diagonal) :]
        for i, ref in enumerate(out_refs[:-1]):
            rows = slice(i * row_count, (i + 1) * row_count)
            total = own[rows]
            for part in sums:
                total = total + part[rows].astype(jnp.float32)
            ref[...] = total.astype(ref.dtype)
        total = last[...]
        for part in sums:
            total = total + part[column_rows:].astype(jnp.float32)
        for part in turns:
            total = total + part[...].astype(jnp.float32)
        out_refs[-1][...] = total

    column_outs = [(shape, jnp.float32)] + [(shape, jnp.bfloat16)] * len(outer) + [(last_shape, jnp.float32)]
    *pieces, half_rows = kernel_call(
        join_columns, column_outs, 1000000, "join_columns", near[0], last_kept, *returned, *last_corners,
    )
    devices = count * lax.axis_size("head")
    vocab = w_vocab.shape[1]

    def vocab_logits(own, other, gain, weight, logits_out, stats_out):
        rows = []
        for part in range(2):
            mine = lax.axis_index("head") == part
            rows.append(jnp.where(mine, own[...], other[...]))
        rows = jnp.concatenate(rows, axis=1)
        scale = lax.rsqrt(jnp.mean(rows * rows, axis=1, keepdims=True) + EPS)
        rows = (rows * scale * gain[...]).astype(jnp.bfloat16)
        largest = None
        for start in range(0, vocab, 512):
            stop = min(start + 512, vocab)
            part = lax.dot_general(
                rows, weight[start:stop, :], (((1,), (1,)), ((), ())), preferred_element_type=jnp.float32
            )
            logits_out[:, start:stop] = part
            top = jnp.max(part, axis=1, keepdims=True)
            largest = top if largest is None else jnp.maximum(largest, top)
        total = jnp.sum(jnp.exp(logits_out[...] - largest), axis=1, keepdims=True)
        row = lax.broadcasted_iota(jnp.int32, (count, 128), 0)
        lane = lax.broadcasted_iota(jnp.int32, (count, 128), 1)
        stats = jnp.where(lane == row, largest, 0.0) + jnp.where(lane == row + 64, total, 0.0)
        stats_out[...] = jnp.broadcast_to(jnp.sum(stats, axis=0)[None, None], stats_out.shape)

    logits, stats = kernel_call(
        vocab_logits, [((count, vocab), jnp.float32), ((devices, 1, 128), jnp.float32)], 2 * count * w_vocab.size,
        "vocab_logits", half_rows, other_core(half_rows), final_gain[None, :],
        pltpu.with_memory_space_constraint(w_vocab.T, pltpu.VMEM),
    )
    corner_sent = []
    if corners:
        corner_outs = [(row_count * i, shape, jnp.bfloat16) for i in range(len(corners))]
        corner_pieces = summed([near[1]] + returned_corners, corner_outs, "corner_sum", gates=(stats,))
        corner_sent = [send(part, count, back(steps)) for part, steps in zip(corner_pieces, diagonal)]
    final = [residual, pieces[0]] + corner_sent + [
        send(part, count, back(steps)) for part, steps in zip(pieces[1:], outer)
    ]
    everyone = lax.all_to_all(stats, ("req", "head"), 0, 0, tiled=True)

    def finish(*refs):
        logits, everyone, hidden_out, log_out = *refs[:2], *refs[-2:]
        total = None
        for ref in refs[2:-2]:
            part = ref[...].astype(jnp.float32)
            total = part if total is None else total + part
        hidden_out[...] = total.astype(jnp.bfloat16)
        tiles = everyone[...]
        top = jnp.max(tiles, axis=0, keepdims=True)
        scaled = jnp.exp(jnp.minimum(tiles - top, 0.0))[:, :64] * tiles[:, 64:]
        spread = jnp.log(jnp.sum(scaled, axis=0, keepdims=True))
        row = lax.broadcasted_iota(jnp.int32, (count, 64), 0)
        lane = lax.broadcasted_iota(jnp.int32, (count, 64), 1)
        largest = jnp.sum(jnp.where(lane == row, top[:, :64], 0.0), axis=1, keepdims=True)
        spread = jnp.sum(jnp.where(lane == row, spread, 0.0), axis=1, keepdims=True)
        log_out[...] = (logits[...] - largest) - spread

    outs = [(shape, jnp.bfloat16), ((count, vocab), jnp.float32)]
    return kernel_call(finish, outs, 1000000, "finish", logits, everyone[:, 0], *final, pinned=False)


def solution(mesh):
    in_specs = (
        P("req", None),
        P(),
        P(None, "head"),
        P(None, "head"),
        P(None, "head"),
        P(),
        P(),
        P("head", None),
        P("req", None, "head"),
        P("req", None, "head"),
        P(),
        P(),
        P("head"),
        P("head", "req"),
        P("head", "req"),
        P("req", "head"),
        P(),
        P(None, ("req", "head")),
    )
    out_specs = (P("req", "head"), P(None, ("req", "head")))
    return jax.shard_map(
        on_device, mesh=mesh, in_specs=in_specs, out_specs=out_specs, check_vma=False
    )
```
